256 devices in a mesh: ctx: 64 (over z, x, core), head: 4 (over y).
Axes of the slice: x: 4, y: 4, z: 8, core: 2. Of those that a mesh axis runs over, the one named last changes fastest.
Arguments:
- queries: bfloat16 [131072, 1024], P('ctx', 'head'), may hold values from -6 to 6
- keys_values: bfloat16 [2, 131072, 1024], P(None, 'ctx', 'head'), may hold values from -6 to 6
- out_weight: bfloat16 [1024, 1024], P('head'), may hold values from -0.1875 to 0.1875
Outputs:
- projected: bfloat16 [131072, 1024], P(('ctx', 'head'))
The draws below stay inside these ranges and needn't reach their ends.
All inputs are finite; a program needn't handle non-finite values.
Results may differ from the reference program's by a relative error of at most 0.012.
The reference program's roundings to bfloat16 on the way (of `pyramid`, `weights` and `attended`) count: a program that leaves them out, or rounds other values in their place, can miss the bound.
Values may be sent and summed in bfloat16 or wider, within the bound.
No kernel may reach another device: no remote copies, remote signals or barrier semaphores. Data moves between devices by JAX's collectives and lax.ppermute only.
A program may use at most 128 MiB of HBM per device.

```python
import math
import jax
import jax.numpy as jnp
from jax import lax

HEADS = 16
HD = 64
D = 1024
BLK = 128
TOKENS = 131072
LOC = 4
LCTX = 6


def draw_queries(key, part):
    key = jax.random.fold_in(key, 11)
    values = jnp.clip(1.4 * jax.random.normal(key, (TOKENS, HEADS * HD), jnp.float32), -6.0, 6.0)
    return values.astype(jnp.bfloat16)


def draw_keys_values(key, part):
    key = jax.random.fold_in(key, 23)
    key_part, value_part = jax.random.split(key)
    keys = jnp.clip(1.4 * jax.random.normal(key_part, (TOKENS, HEADS * HD), jnp.float32), -6.0, 6.0)
    values = jnp.clip(jax.random.normal(value_part, (TOKENS, HEADS * HD), jnp.float32), -6.0, 6.0)
    return jnp.stack([keys, values]).astype(jnp.bfloat16)


def level_of(rng, extent, cuts, smallest, top_value):
    gain, own = 1.0, jax.random.fold_in(rng, 6)
    for dim, blocks in cuts:
        heights = jnp.exp(jax.random.uniform(jax.random.fold_in(own, dim), (blocks,), jnp.float32, smallest / len(cuts), top_value / len(cuts)))
        gain = gain * jnp.repeat(heights, extent[dim] // blocks).reshape([-1 if axis == dim else 1 for axis in range(len(extent))])
    return gain


def noise(rng, shape, scale, limit, cuts=(), kind=jnp.bfloat16):
    entries = scale * jax.random.normal(rng, shape, jnp.float32)
    if cuts:
        entries = entries * level_of(rng, shape, cuts, -0.22, 0.18)
    return jnp.clip(entries, -limit, limit).astype(kind)


def setup_inputs(seed: int = 0) -> dict:
    key_of = jax.random.split(jax.random.key(seed), 4)
    queries = draw_queries(jax.random.fold_in(key_of[3], 71), 0)
    keys_values = draw_keys_values(jax.random.fold_in(key_of[3], 71), 0)
    out_weight = noise(key_of[2], (D, D), D ** -0.5, 0.1875, ((0, 4),))
    return {"queries": queries, "keys_values": keys_values, "out_weight": out_weight}


def coarsen(keyval):
    pairs = keyval.astype(jnp.float32).reshape(keyval.shape[0], keyval.shape[1] // 2, 2, keyval.shape[2])
    return ((pairs[:, :, 0] + pairs[:, :, 1]) * (1.0 / math.sqrt(2.0))).astype(jnp.bfloat16)

def reference(queries, keys_values, out_weight):
    width = HEADS * HD
    nblocks = TOKENS // BLK
    levels = LOC + LCTX - 1
    pyramid = [keys_values]
    for level in range(levels):
        pyramid.append(coarsen(pyramid[-1]))
    padded = jnp.pad(keys_values, ((0, 0), (BLK, BLK), (0, 0)))
    group = 8
    scale = HD ** (-0.5)
    keycount = (3 + levels) * BLK
    column = jnp.arange(keycount, dtype=jnp.int32)

    def keys_for(block):
        parts = [lax.dynamic_slice_in_dim(padded, block * BLK, 3 * BLK, 1)]
        for level in range(1, levels + 1):
            start = (jnp.bitwise_xor(jnp.right_shift(block, level), 1) * BLK).astype(jnp.int32)
            parts.append(lax.dynamic_slice_in_dim(pyramid[level], start, BLK, 1))
        return jnp.concatenate(parts, 1)

    def one_group(index):
        blocks = index * group + jnp.arange(group, dtype=jnp.int32)
        sets = jax.vmap(keys_for)(blocks).reshape(group, 2, keycount, HEADS, HD).astype(jnp.float32)
        rows = lax.dynamic_slice_in_dim(queries, (index * group * BLK).astype(jnp.int32), group * BLK, 0)
        rows = rows.reshape(group, BLK, HEADS, HD).astype(jnp.float32)
        scores = jnp.einsum('gqhd,gkhd->ghqk', rows, sets[:, 0]) * scale
        lower = (column[None, :] >= BLK) | (blocks[:, None] >= 1)
        upper = (column[None, :] < 2 * BLK) | (column[None, :] >= 3 * BLK) | (blocks[:, None] + 1 < nblocks)
        valid = lower & upper
        scores = jnp.where(valid[:, None, None, :], scores, -jnp.inf)
        top = lax.optimization_barrier(jnp.max(scores, axis=-1, keepdims=True))
        expo = jnp.exp(scores - top)
        weights = (expo / lax.optimization_barrier(jnp.sum(expo, axis=-1, keepdims=True))).astype(jnp.bfloat16)
        attended = jnp.einsum('ghqk,gkhd->gqhd', weights.astype(jnp.float32), sets[:, 1])
        return attended.astype(jnp.bfloat16).reshape(group * BLK, width)
    attended = lax.map(one_group, jnp.arange(nblocks // group, dtype=jnp.int32)).reshape(TOKENS, width)
    return jnp.dot(attended, out_weight, preferred_element_type=jnp.float32).astype(jnp.bfloat16)
```

```python
import functools
import math

import jax
import jax.numpy as jnp
from jax import lax
from jax.experimental import pallas as pl
from jax.experimental.pallas import tpu as pltpu
from jax.sharding import PartitionSpec as P

HD = 64
BLK = 128
WIDE = 256
CHUNK = 512
SCALE = math.log2(math.e) / math.sqrt(HD)
ROOT = 1.0 / math.sqrt(2.0)
HIDE = -1e30
NT = (((1,), (1,)), ((), ()))
F32 = jnp.float32
BF16 = jnp.bfloat16

VMEM = pl.BlockSpec(memory_space=pltpu.VMEM)
SMEM = pl.BlockSpec(memory_space=pltpu.SMEM)


def call(kernel, name, outs, args, n_scalar=1, limit=24):
    return list(pl.pallas_call(
        kernel,
        out_shape=[jax.ShapeDtypeStruct(shape, dtype) for shape, dtype in outs],
        in_specs=[SMEM] * n_scalar + [VMEM] * (len(args) - n_scalar),
        out_specs=[VMEM] * len(outs),
        compiler_params=pltpu.CompilerParams(vmem_limit_bytes=limit * 2**20),
        name=name,
    )(*args))


def halve(rows):
    n = rows.shape[0]
    out = lax.broadcasted_iota(jnp.int32, (n // 2, n), 0)
    col = lax.broadcasted_iota(jnp.int32, (n // 2, n), 1)
    pairs = (col // 2 == out).astype(BF16)
    return (jnp.dot(pairs, rows, preferred_element_type=F32) * ROOT).astype(BF16)


def pyramid_kernel(kv_ref, pyr_ref, top_ref):
    for side in range(2):
        for i in range(8):
            pyr_ref[side, pl.ds(i * 128, 128)] = halve(kv_ref[side, pl.ds(i * 256, 256)])
    for side in range(2):
        for i in range(4):
            pyr_ref[side, pl.ds(1024 + i * 128, 128)] = halve(pyr_ref[side, pl.ds(i * 256, 256)])
    for side in range(2):
        for i in range(2):
            pyr_ref[side, pl.ds(1536 + i * 128, 128)] = halve(
                pyr_ref[side, pl.ds(1024 + i * 256, 256)]
            )
    for side in range(2):
        top_ref[side] = halve(pyr_ref[side, pl.ds(1536, 256)])


def climb_kernel(at_ref, mine_ref, other_ref, up_ref):
    side, bit = at_ref[0], at_ref[1]
    if len(mine_ref.shape) == 3:
        mine, other = mine_ref[side], other_ref[side]
    else:
        mine, other = mine_ref[...], other_ref[...]
    mine, other = halve(mine), halve(other)
    low = bit == 0
    up_ref[pl.ds(0, 64)] = jnp.where(low, mine, other)
    up_ref[pl.ds(64, 64)] = jnp.where(low, other, mine)


def near_kernel(at_ref, q_ref, kv_ref, pyr_ref, low_ref, high_ref, o_ref, ml_ref):
    chunk, low_bias_on, high_bias_on = at_ref[0], at_ref[1], at_ref[2]
    lane = lax.broadcasted_iota(jnp.int32, (256, WIDE), 1) // HD
    slot = lax.broadcasted_iota(jnp.int32, (256, 128), 1) // 16
    zero = jnp.zeros((256, WIDE), BF16)

    def panel(ref, side, start, rows=BLK):
        return ref[side, pl.ds(pl.multiple_of(start, BLK), rows)]

    for t in range(2):
        base = chunk * CHUNK + t * 256
        q = q_ref[pl.ds(pl.multiple_of(base, 256), 256)]
        parts = []
        for side in range(2):
            main = jnp.concatenate(
                [
                    panel(kv_ref, side, base, 256),
                    panel(pyr_ref, side, chunk * 256 + (1 - t) * BLK),
                    panel(pyr_ref, side, 1024 + jnp.bitwise_xor(chunk, 1) * BLK),
                ],
                0,
            )
            third = panel(pyr_ref, side, 1536 + jnp.bitwise_xor(lax.shift_right_logical(chunk, 1), 1) * BLK)
            if t == 0:
                low = panel(kv_ref, side, jnp.maximum(base - BLK, 0))
                low = jnp.where(chunk == 0, low_ref[side], low)
                high = panel(kv_ref, side, base + 256)
            else:
                low = panel(kv_ref, side, base - BLK)
                high = panel(kv_ref, side, jnp.minimum(base + 256, 2048 - BLK))
                high = jnp.where(chunk == 3, high_ref[side], high)
            parts.append((main, jnp.concatenate([third, low], 0), jnp.concatenate([third, high], 0)))
        (k1, k2, k3), (v1, v2, v3) = parts
        out = jnp.zeros((256, WIDE), F32)
        ml = jnp.zeros((256, 128), F32)
        for h in range(4):
            qh = jnp.where(lane == h, q, zero)
            s1 = lax.dot_general(qh, k1, NT, preferred_element_type=F32)
            s2 = lax.dot_general(qh[:128], k2, NT, preferred_element_type=F32)
            s3 = lax.dot_general(qh[128:], k3, NT, preferred_element_type=F32)
            if t == 0:
                bias = jnp.where((chunk == 0) & (low_bias_on == 1), HIDE, 0.0)
                s2 = jnp.concatenate([s2[:, :128], s2[:, 128:] + bias], 1)
            else:
                bias = jnp.where((chunk == 3) & (high_bias_on == 1), HIDE, 0.0)
                s3 = jnp.concatenate([s3[:, :128], s3[:, 128:] + bias], 1)
            s23 = jnp.concatenate([s2, s3], 0)
            m = jnp.maximum(
                jnp.max(s1, axis=1, keepdims=True), jnp.max(s23, axis=1, keepdims=True)
            )
            p1 = jnp.exp2((s1 - m) * SCALE)
            p23 = jnp.exp2((s23 - m) * SCALE)
            total = jnp.sum(p1, axis=1, keepdims=True) + jnp.sum(p23, axis=1, keepdims=True)
            p1, p23 = p1.astype(BF16), p23.astype(BF16)
            o = jnp.dot(p1, v1, preferred_element_type=F32)
            o = o + jnp.concatenate(
                [
                    jnp.dot(p23[:128], v2, preferred_element_type=F32),
                    jnp.dot(p23[128:], v3, preferred_element_type=F32),
                ],
                0,
            )
            out = jnp.where(lane == h, o, out)
            ml = jnp.where(slot == 2 * h, m, jnp.where(slot == 2 * h + 1, total, ml))
        o_ref[pl.ds(t * 256, 256)] = out
        ml_ref[pl.ds(t * 256, 256)] = ml


def far_kernel(at_ref, q_ref, o_ref, ml_ref, sib_ref, mine_ref, other_ref, out_ref):
    chunk, core = at_ref[0], at_ref[3]
    lane = lax.broadcasted_iota(jnp.int32, (CHUNK, WIDE), 1) // HD
    q = q_ref[pl.ds(pl.multiple_of(chunk * CHUNK, CHUNK), CHUNK)]
    first = core == 0
    mine, other = mine_ref[...].reshape(5 * BLK, WIDE), other_ref[...].reshape(5 * BLK, WIDE)
    k = jnp.concatenate([sib_ref[0], jnp.where(first, mine, other)], 0)
    v = jnp.concatenate([sib_ref[1], jnp.where(first, other, mine)], 0)
    zero = jnp.zeros_like(q)
    out = jnp.zeros((CHUNK, WIDE), F32)
    for h in range(4):
        qh = jnp.where(lane == h, q, zero)
        s = lax.dot_general(qh, k, NT, preferred_element_type=F32)
        before = ml_ref[:, 32 * h : 32 * h + 1]
        total = ml_ref[:, 32 * h + 16 : 32 * h + 17]
        m = jnp.maximum(jnp.max(s, axis=1, keepdims=True), before)
        keep = jnp.exp2((before - m) * SCALE)
        p = jnp.exp2((s - m) * SCALE)
        total = total * keep + jnp.sum(p, axis=1, keepdims=True)
        o = jnp.dot(p.astype(BF16), v, preferred_element_type=F32)
        o = (o + o_ref[...] * keep) * (1.0 / total)
        out = jnp.where(lane == h, o, out)
    out_ref[...] = out.astype(BF16)


def project_kernel(at_ref, *refs):
    core = at_ref[3]
    atts, w_own, w_mine, w_other, out_ref = refs[:4], refs[4], refs[5], refs[6], refs[7]
    for half in range(2):
        cols = pl.ds(half * 512, 512)
        total = jnp.dot(atts[0][...], w_own[:, cols], preferred_element_type=F32)
        for i in range(3):
            w = jnp.where(core == half, w_mine[i], w_other[i])
            total = total + jnp.dot(atts[i + 1][...], w, preferred_element_type=F32)
        out_ref[:, cols] = total.astype(BF16)


def body(queries, keys_values, out_weight):
    shards = lax.axis_size("ctx")
    heads = lax.axis_size("head")
    place = lax.axis_index("ctx")
    rank = lax.axis_index("head")
    core = jnp.bitwise_and(place, 1)

    def swap(x, bit):
        return lax.ppermute(x, "ctx", [(i, i ^ bit) for i in range(shards)])

    def turn(x, by):
        return lax.ppermute(x, "head", [(i, (i + by) % heads) for i in range(heads)])

    forward = [(i, i + 1) for i in range(shards - 1)]
    backward = [(b, a) for a, b in forward]
    low = lax.ppermute(lax.slice_in_dim(keys_values, 2048 - BLK, 2048, axis=1), "ctx", forward)
    high = lax.ppermute(lax.slice_in_dim(keys_values, 0, BLK, axis=1), "ctx", backward)

    pyr, top = call(
        pyramid_kernel,
        "pyramid",
        [((2, 1792, WIDE), BF16), ((2, BLK, WIDE), BF16)],
        (keys_values,),
        n_scalar=0,
    )

    turns = (2, 1, 3, 0)
    at = [
        jnp.stack(
            [
                (rank + by) % heads,
                (place == 0).astype(jnp.int32),
                (place == shards - 1).astype(jnp.int32),
                core,
            ]
        ).astype(jnp.int32)
        for by in turns
    ]

    sibling = swap(top, 1)
    w_half = lax.dynamic_slice_in_dim(out_weight, core * 512, 512, 1)
    near = []
    panels = []
    mine, other = top, sibling
    w_parts = None
    for step in range(1, 6):
        if step <= 4:
            gate = queries if step == 1 else lax.optimization_barrier((queries, mine))[0]
            near.append(
                call(
                    near_kernel,
                    "near",
                    [((CHUNK, WIDE), F32), ((CHUNK, 128), F32)],
                    (at[step - 1], gate, keys_values, pyr, low, high),
                )
            )
            other, last = lax.optimization_barrier((other, near[-1][0]))
            near[-1][0] = last
        bit = jnp.bitwise_and(lax.shift_right_logical(place, step - 1), 1)
        up = jnp.stack([core, bit]).astype(jnp.int32)
        (mine,) = call(climb_kernel, "climb", [((BLK, WIDE), BF16)], (up, mine, other))
        other = swap(mine, 1 << step)
        panels.append(other)
        if step == 1:
            gated = lax.optimization_barrier((w_half, mine))[0]
            w_parts = jnp.stack([turn(gated, by) for by in turns[:3]])
    held = jnp.stack(panels)
    theirs = swap(held, 1)
    w_theirs = swap(w_parts, 1)
    atts = []
    for i, by in enumerate(turns):
        (att,) = call(
            far_kernel,
            "far",
            [((CHUNK, WIDE), BF16)],
            (at[i], queries, near[i][0], near[i][1], sibling, held, theirs),
        )
        atts.append(turn(att, by) if by else att)
    (out,) = call(
        project_kernel,
        "project",
        [((CHUNK, 1024), BF16)],
        (at[0], atts[3], atts[0], atts[1], atts[2], out_weight, w_parts, w_theirs),
    )
    return out


def solution(mesh):
    in_specs = (P("ctx", "head"), P(None, "ctx", "head"), P("head", None))
    out_specs = P(("ctx", "head"), None)
    return jax.shard_map(body, mesh=mesh, in_specs=in_specs, out_specs=out_specs, check_vma=False)
```

```python
import functools
import math

import jax
import jax.numpy as jnp
from jax import lax
from jax.experimental import pallas as pl
from jax.experimental.pallas import tpu as pltpu
from jax.sharding import PartitionSpec as P

HD = 64
BLK = 128
WIDE = 256
CHUNK = 512
SCALE = math.log2(math.e) / math.sqrt(HD)
ROOT = 1.0 / math.sqrt(2.0)
HIDE = -1e30
NT = (((1,), (1,)), ((), ()))
F32 = jnp.float32
BF16 = jnp.bfloat16

VMEM = pl.BlockSpec(memory_space=pltpu.VMEM)
SMEM = pl.BlockSpec(memory_space=pltpu.SMEM)


def call(kernel, name, outs, args, n_scalar=1, limit=16):
    return list(pl.pallas_call(
        kernel,
        out_shape=[jax.ShapeDtypeStruct(shape, dtype) for shape, dtype in outs],
        in_specs=[SMEM] * n_scalar + [VMEM] * (len(args) - n_scalar),
        out_specs=[VMEM] * len(outs),
        compiler_params=pltpu.CompilerParams(vmem_limit_bytes=limit * 2**20),
        name=name,
    )(*args))


def halve(rows):
    n = rows.shape[0]
    out = lax.broadcasted_iota(jnp.int32, (n // 2, n), 0)
    col = lax.broadcasted_iota(jnp.int32, (n // 2, n), 1)
    pairs = (col // 2 == out).astype(BF16)
    return (jnp.dot(pairs, rows, preferred_element_type=F32) * ROOT).astype(BF16)


def spread(q, pair):
    x = q[:, pair * 128 : pair * 128 + 128].astype(F32) * SCALE
    head = x.astype(BF16)
    rest = (x - head.astype(F32)).astype(BF16)
    low = lax.broadcasted_iota(jnp.int32, head.shape, 1) < HD
    zero = jnp.zeros_like(head)
    return [
        jnp.concatenate([jnp.where(keep, head, zero), jnp.where(keep, rest, zero)], 1)
        for keep in (low, jnp.logical_not(low))
    ]


def twice(k, pair):
    k = k[:, pair * 128 : pair * 128 + 128]
    return jnp.concatenate([k, k], 1)


def ones_beside(v, pair):
    v = v[:, pair * 128 : pair * 128 + 128]
    return jnp.concatenate([v, jnp.ones_like(v)], 1)


def scores(q, k):
    return lax.dot_general(q, k, NT, preferred_element_type=F32)


def select(x0, x1):
    low = lax.broadcasted_iota(jnp.int32, (x0.shape[0], 128), 1) < HD
    return jnp.where(low, x0, x1)


def pyramid_kernel(at_ref, kv_ref, pyr_ref, face_ref, back_ref):
    even = jnp.bitwise_and(at_ref[1], 1) == 0
    for side in range(2):
        for i in range(8):
            pyr_ref[side, pl.ds(i * 128, 128)] = halve(kv_ref[side, pl.ds(i * 256, 256)])
        first, last = kv_ref[side, pl.ds(0, BLK)], kv_ref[side, pl.ds(2048 - BLK, BLK)]
        face_ref[side, pl.ds(BLK, BLK)] = jnp.where(even, last, first)
        back_ref[side] = jnp.where(even, first, last)
    for side in range(2):
        for i in range(4):
            pyr_ref[side, pl.ds(1024 + i * 128, 128)] = halve(pyr_ref[side, pl.ds(i * 256, 256)])
    for side in range(2):
        for i in range(2):
            pyr_ref[side, pl.ds(1536 + i * 128, 128)] = halve(
                pyr_ref[side, pl.ds(1024 + i * 256, 256)]
            )
    for side in range(2):
        face_ref[side, pl.ds(0, BLK)] = halve(pyr_ref[side, pl.ds(1536, 256)])


def climb_kernel(step, at_ref, mine_ref, other_ref, up_ref):
    place = at_ref[1]
    low = jnp.bitwise_and(lax.shift_right_logical(place, step - 1), 1) == 0
    if step == 1:
        side = jnp.bitwise_and(place, 1)
        mine, other = mine_ref[side, pl.ds(0, BLK)], other_ref[side, pl.ds(0, BLK)]
    else:
        mine, other = mine_ref[...], other_ref[...]
    mine, other = halve(mine), halve(other)
    up_ref[pl.ds(0, 64)] = jnp.where(low, mine, other)
    up_ref[pl.ds(64, 64)] = jnp.where(low, other, mine)


def near_kernel(by, shards, at_ref, q_ref, kv_ref, pyr_ref, face_ref, back_ref, o_ref, l_ref, m_ref):
    chunk, place = jnp.bitwise_and(at_ref[0] + by, 3), at_ref[1]
    even = jnp.bitwise_and(place, 1) == 0

    def panel(ref, side, start, rows=BLK):
        return ref[side, pl.ds(pl.multiple_of(start, BLK), rows)]
    for t in range(2):
        base = chunk * CHUNK + t * 256
        q = q_ref[pl.ds(pl.multiple_of(base, 256), 256)]
        parts = []
        for side in range(2):
            main = jnp.concatenate([
                panel(kv_ref, side, base, 256),
                panel(pyr_ref, side, chunk * 256 + (1 - t) * BLK),
                panel(pyr_ref, side, 1024 + jnp.bitwise_xor(chunk, 1) * BLK)], 0)
            third = panel(pyr_ref, side, 1536 + jnp.bitwise_xor(lax.shift_right_logical(chunk, 1), 1) * BLK)
            if t == 0:
                low = panel(kv_ref, side, jnp.maximum(base - BLK, 0))
                halo = jnp.where(even, back_ref[side], face_ref[side, pl.ds(BLK, BLK)])
                low = jnp.where(chunk == 0, halo, low)
                high = panel(kv_ref, side, base + 256)
            else:
                low = panel(kv_ref, side, base - BLK)
                high = panel(kv_ref, side, jnp.minimum(base + 256, 2048 - BLK))
                halo = jnp.where(even, face_ref[side, pl.ds(BLK, BLK)], back_ref[side])
                high = jnp.where(chunk == 3, halo, high)
            parts.append((main, jnp.concatenate([third, low], 0), jnp.concatenate([third, high], 0)))
        ks, vs = parts
        for pair in range(2):
            h0, h1 = spread(q, pair)
            qs = jnp.concatenate([h0[:128], h1[:128], h0[128:], h1[128:]], 0)
            k1, k2, k3 = [twice(k, pair) for k in ks]
            v1, v2, v3 = [ones_beside(v, pair) for v in vs]
            s1 = scores(qs, k1)
            s2 = scores(qs[:256], k2)
            s3 = scores(qs[256:], k3)
            if t == 0:
                bias = jnp.where((chunk == 0) & (place == 0), HIDE, 0.0)
                s2 = jnp.concatenate([s2[:, :128], s2[:, 128:] + bias], 1)
            else:
                bias = jnp.where((chunk == 3) & (place == shards - 1), HIDE, 0.0)
                s3 = jnp.concatenate([s3[:, :128], s3[:, 128:] + bias], 1)
            s23 = jnp.concatenate([s2, s3], 0)
            m = jnp.max(jnp.concatenate([s1, s23], 1), axis=1, keepdims=True)
            p1 = jnp.exp2(s1 - m).astype(BF16)
            p23 = jnp.exp2(s23 - m).astype(BF16)
            o = jnp.dot(p1, v1, preferred_element_type=F32)
            o = o + jnp.concatenate([jnp.dot(p23[:256], v2, preferred_element_type=F32),
                                     jnp.dot(p23[256:], v3, preferred_element_type=F32)], 0)
            for part in range(2):
                r = part * 256
                rows = pl.ds(t * 256 + part * 128, 128)
                cols = pl.ds(pair * 128, 128)
                o_ref[rows, cols] = select(o[r:r+128, :128], o[r+128:r+256, :128])
                l_ref[rows, cols] = select(o[r:r+128, 128:], o[r+128:r+256, 128:])
                m_ref[rows, cols] = select(m[r:r+128], m[r+128:r+256])


def far_kernel(by, at_ref, q_ref, o_ref, l_ref, m_ref, face_ref, mine_ref, other_ref, out_ref):
    chunk, core = jnp.bitwise_and(at_ref[0] + by, 3), jnp.bitwise_and(at_ref[1], 1)
    q = q_ref[pl.ds(pl.multiple_of(chunk * CHUNK, CHUNK), CHUNK)]
    mine, other = mine_ref[...].reshape(5 * BLK, WIDE), other_ref[...].reshape(5 * BLK, WIDE)
    k = jnp.concatenate([face_ref[0, pl.ds(0, BLK)], jnp.where(core == 0, mine, other)], 0)
    v = jnp.concatenate([face_ref[1, pl.ds(0, BLK)], jnp.where(core == 0, other, mine)], 0)
    for pair in range(2):
        k1, v1 = twice(k, pair), ones_beside(v, pair)
        sums, tops = [], []
        for qh in spread(q, pair):
            s = scores(qh, k1)
            m = jnp.max(s, axis=1, keepdims=True)
            sums.append(jnp.dot(jnp.exp2(s - m).astype(BF16), v1, preferred_element_type=F32))
            tops.append(m)
        cols = pl.ds(pair * 128, 128)
        o = select(sums[0][:, :128], sums[1][:, :128])
        l = select(sums[0][:, 128:], sums[1][:, 128:])
        m = select(*tops)
        before = m_ref[:, cols]
        top = jnp.maximum(m, before)
        a, b = jnp.exp2(before - top), jnp.exp2(m - top)
        out = (o * b + o_ref[:, cols] * a) / (l * b + l_ref[:, cols] * a)
        out_ref[:, cols] = out.astype(BF16)


def project_kernel(*refs):
    out_ref = refs[8]
    total = jnp.dot(refs[0][...], refs[4][...], preferred_element_type=F32)
    for i in range(1, 4):
        total = total + jnp.dot(refs[i][...], refs[4 + i][...], preferred_element_type=F32)
    out_ref[...] = total.astype(BF16)


def body(queries, keys_values, out_weight):
    shards = lax.axis_size("ctx")
    heads = lax.axis_size("head")
    place = lax.axis_index("ctx")
    rank = lax.axis_index("head")
    at = jnp.stack([rank, place]).astype(jnp.int32)

    def swap(x, bits):
        return lax.ppermute(x, "ctx", [(i, i ^ bits) for i in range(shards)])

    def turn(x, by):
        return lax.ppermute(x, "head", [(i, (i + by) % heads) for i in range(heads)])

    pyr, face, back = call(
        pyramid_kernel,
        "pyramid",
        [((2, 1792, WIDE), BF16), ((2, 2 * BLK, WIDE), BF16), ((2, BLK, WIDE), BF16)],
        (at, keys_values),
    )
    turns = (3, 1, 2, 0)
    sibling = swap(face, 1)
    ends = [(i, i + 1) for i in range(1, shards - 1, 2)]
    back = lax.ppermute(back, "ctx", ends + [(b, a) for a, b in ends])
    near, panels = [], []
    mine, other = face, sibling
    weights = [turn(out_weight, by) for by in turns[:3]]
    for step, bits in enumerate((2, 6, 8, 16, 56), 1):
        if step == 4:
            other, weights[0] = lax.optimization_barrier((other, weights[0]))
        if step == 5:
            other, *weights = lax.optimization_barrier((other, *weights))
        (mine,) = call(
            functools.partial(climb_kernel, step), "climb", [((BLK, WIDE), BF16)], (at, mine, other)
        )
        other = swap(mine, bits)
        if step <= 4:
            gate = lax.optimization_barrier((queries, mine))[0]
            state = call(
                functools.partial(near_kernel, turns[step - 1], shards),
                "near",
                [((CHUNK, WIDE), F32)] * 3,
                (at, gate, keys_values, pyr, sibling, back),
            )
            other, state[0] = lax.optimization_barrier((other, state[0]))
            near.append(state)
        panels.append(other)
    held = jnp.stack(panels)
    theirs = swap(held, 1)
    atts = []
    for by, state in zip(turns, near):
        (att,) = call(
            functools.partial(far_kernel, by),
            "far",
            [((CHUNK, WIDE), BF16)],
            (at, queries, *state, sibling, held, theirs),
        )
        atts.append(turn(att, by) if by else att)
    (out,) = call(
        project_kernel, "project", [((CHUNK, 1024), BF16)], (*atts, *weights, out_weight), n_scalar=0
    )
    return out


def solution(mesh):
    in_specs = (P("ctx", "head"), P(None, "ctx", "head"), P("head", None))
    out_specs = P(("ctx", "head"), None)
    return jax.shard_map(body, mesh=mesh, in_specs=in_specs, out_specs=out_specs, check_vma=False)
```

```python
import functools
import math

import jax
import jax.numpy as jnp
from jax import lax
from jax.experimental import pallas as pl
from jax.experimental.pallas import tpu as pltpu
from jax.sharding import PartitionSpec as P

HD = 64
BLK = 128
WIDE = 256
CHUNK = 512
SCALE = math.log2(math.e) / math.sqrt(HD)
ROOT = 1.0 / math.sqrt(2.0)
HIDE = -1e30
NT = (((1,), (1,)), ((), ()))
F32 = jnp.float32
BF16 = jnp.bfloat16

VMEM = pl.BlockSpec(memory_space=pltpu.VMEM)
SMEM = pl.BlockSpec(memory_space=pltpu.SMEM)


def call(kernel, name, outs, args, after=(), limit=16):
    n, late = len(args), len(after)
    return list(
        pl.pallas_call(
            lambda *refs: kernel(*refs[:n], *refs[n + late :]),
            out_shape=[jax.ShapeDtypeStruct(shape, dtype) for shape, dtype in outs],
            in_specs=[SMEM] + [VMEM] * (n - 1) + [pl.BlockSpec(memory_space=pl.ANY)] * late,
            out_specs=[VMEM] * len(outs),
            compiler_params=pltpu.CompilerParams(vmem_limit_bytes=limit * 2**20),
            name=name,
        )(*args, *after)
    )


def halve(rows):
    n = rows.shape[0]
    out = lax.broadcasted_iota(jnp.int32, (n // 2, n), 0)
    col = lax.broadcasted_iota(jnp.int32, (n // 2, n), 1)
    pairs = (col // 2 == out).astype(BF16)
    return (jnp.dot(pairs, rows, preferred_element_type=F32) * ROOT).astype(BF16)


def spread(q, pair):
    x = q[:, pair * 128 : pair * 128 + 128].astype(F32) * SCALE
    head = x.astype(BF16)
    rest = (x - head.astype(F32)).astype(BF16)
    low = lax.broadcasted_iota(jnp.int32, head.shape, 1) < HD
    zero = jnp.zeros_like(head)
    return [
        jnp.concatenate([jnp.where(keep, head, zero), jnp.where(keep, rest, zero)], 1)
        for keep in (low, jnp.logical_not(low))
    ]


def twice(k, pair):
    k = k[:, pair * 128 : pair * 128 + 128]
    return jnp.concatenate([k, k], 1)


def ones_beside(v, pair):
    v = v[:, pair * 128 : pair * 128 + 128]
    return jnp.concatenate([v, jnp.ones_like(v)], 1)


def scores(q, k):
    return lax.dot_general(q, k, NT, preferred_element_type=F32)


def select(x0, x1):
    low = lax.broadcasted_iota(jnp.int32, (x0.shape[0], 128), 1) < HD
    return jnp.where(low, x0, x1)


def pyramid_kernel(at_ref, kv_ref, q_ref, lev_ref, face_ref, back_ref):
    even = jnp.bitwise_and(at_ref[1], 1) == 0
    for side in range(2):
        for i in range(8):
            rows = kv_ref[side, pl.ds(i * 256, 256)]
            lev_ref[side, pl.ds(i * 256, 256)] = rows
            lev_ref[side, pl.ds(2048 + i * 128, 128)] = halve(rows)
        first, last = kv_ref[side, pl.ds(0, BLK)], kv_ref[side, pl.ds(2048 - BLK, BLK)]
        face_ref[side, pl.ds(BLK, BLK)] = jnp.where(even, last, first)
        back_ref[side] = jnp.where(even, first, last)
    for side in range(2):
        for i in range(4):
            lev_ref[side, pl.ds(3072 + i * 128, 128)] = halve(lev_ref[side, pl.ds(2048 + i * 256, 256)])
    for side in range(2):
        for i in range(2):
            lev_ref[side, pl.ds(3584 + i * 128, 128)] = halve(lev_ref[side, pl.ds(3072 + i * 256, 256)])
    for side in range(2):
        face_ref[side, pl.ds(0, BLK)] = halve(lev_ref[side, pl.ds(3584, 256)])


def bit_of(at_ref, bit):
    return jnp.bitwise_and(lax.shift_right_logical(at_ref[1], bit), 1) == 0


def ordered(low, mine, other):
    return jnp.concatenate([jnp.where(low, mine, other), jnp.where(low, other, mine)], 0)


def start_kernel(at_ref, mine_ref, other_ref, up_ref, half_ref):
    side = jnp.bitwise_and(at_ref[1], 1)
    up = ordered(
        bit_of(at_ref, 0), halve(mine_ref[side, pl.ds(0, BLK)]), halve(other_ref[side, pl.ds(0, BLK)])
    )
    up_ref[...] = up
    half_ref[...] = halve(up)


def climb(bit, at_ref, mine_ref, near_ref, same_ref, cross_ref):
    low = bit_of(at_ref, bit)
    own = ordered(low, halve(mine_ref[...]), halve(near_ref[...]))
    sibling = ordered(low, same_ref[...], cross_ref[...])
    return sibling, ordered(bit_of(at_ref, bit + 1), halve(own), halve(sibling))


def middle_kernel(at_ref, mine_ref, near_ref, same_ref, cross_ref, w_ref, sib_ref, up_ref, half_ref, w_half_ref):
    sib_ref[...], up = climb(1, at_ref, mine_ref, near_ref, same_ref, cross_ref)
    up_ref[...] = up
    half_ref[...] = halve(up)
    core = jnp.bitwise_and(at_ref[1], 1)
    w_half_ref[...] = w_ref[pl.ds(pl.multiple_of(core * 128, 128), 128)]


def last_kernel(at_ref, mine_ref, near_ref, same_ref, cross_ref, p5_ref, p6_ref, up_ref, held_ref):
    held_ref[0], held_ref[1], held_ref[2] = p5_ref[...], p6_ref[...], near_ref[...]
    held_ref[3], up_ref[...] = climb(3, at_ref, mine_ref, near_ref, same_ref, cross_ref)


def near_chunk(by, shards, at_ref, q_ref, lev_ref, face_ref, back_ref, o_ref, l_ref, m_ref):
    chunk, place = jnp.bitwise_and(at_ref[0] + by, 3), at_ref[1]
    even = jnp.bitwise_and(place, 1) == 0

    def panel(ref, side, start, rows=BLK):
        return ref[side, pl.ds(pl.multiple_of(start, BLK), rows)]
    for t in range(2):
        base = chunk * CHUNK + t * 256
        q = q_ref[pl.ds(pl.multiple_of(base, 256), 256)]
        parts = []
        for side in range(2):
            main = jnp.concatenate([
                panel(lev_ref, side, base, 256),
                panel(lev_ref, side, 2048 + chunk * 256 + (1 - t) * BLK),
                panel(lev_ref, side, 3072 + jnp.bitwise_xor(chunk, 1) * BLK)], 0)
            third = panel(lev_ref, side, 3584 + jnp.bitwise_xor(lax.shift_right_logical(chunk, 1), 1) * BLK)
            if t == 0:
                low = panel(lev_ref, side, jnp.maximum(base - BLK, 0))
                halo = jnp.where(even, back_ref[side], face_ref[side, pl.ds(BLK, BLK)])
                low = jnp.where(chunk == 0, halo, low)
                high = panel(lev_ref, side, base + 256)
            else:
                low = panel(lev_ref, side, base - BLK)
                high = panel(lev_ref, side, jnp.minimum(base + 256, 2048 - BLK))
                halo = jnp.where(even, face_ref[side, pl.ds(BLK, BLK)], back_ref[side])
                high = jnp.where(chunk == 3, halo, high)
            parts.append((main, jnp.concatenate([third, low], 0), jnp.concatenate([third, high], 0)))
        ks, vs = parts
        for pair in range(2):
            h0, h1 = spread(q, pair)
            qs = jnp.concatenate([h0[:128], h1[:128], h0[128:], h1[128:]], 0)
            k1, k2, k3 = [twice(k, pair) for k in ks]
            v1, v2, v3 = [ones_beside(v, pair) for v in vs]
            s1 = scores(qs, k1)
            s2 = scores(qs[:256], k2)
            s3 = scores(qs[256:], k3)
            if t == 0:
                bias = jnp.where((chunk == 0) & (place == 0), HIDE, 0.0)
                s2 = jnp.concatenate([s2[:, :128], s2[:, 128:] + bias], 1)
            else:
                bias = jnp.where((chunk == 3) & (place == shards - 1), HIDE, 0.0)
                s3 = jnp.concatenate([s3[:, :128], s3[:, 128:] + bias], 1)
            s23 = jnp.concatenate([s2, s3], 0)
            m = jnp.max(jnp.concatenate([s1, s23], 1), axis=1, keepdims=True)
            p1 = jnp.exp2(s1 - m).astype(BF16)
            p23 = jnp.exp2(s23 - m).astype(BF16)
            o = jnp.dot(p1, v1, preferred_element_type=F32)
            o = o + jnp.concatenate([jnp.dot(p23[:256], v2, preferred_element_type=F32),
                                     jnp.dot(p23[256:], v3, preferred_element_type=F32)], 0)
            for part in range(2):
                r = part * 256
                rows = pl.ds(t * 256 + part * 128, 128)
                cols = pl.ds(pair * 128, 128)
                o_ref[rows, cols] = select(o[r:r+128, :128], o[r+128:r+256, :128])
                l_ref[rows, cols] = select(o[r:r+128, 128:], o[r+128:r+256, 128:])
                m_ref[rows, cols] = select(m[r:r+128], m[r+128:r+256])


def near_kernel(turns, shards, *refs):
    for i, by in enumerate(turns):
        near_chunk(by, shards, *refs[:5], *refs[5 + 3 * i : 8 + 3 * i])


def far_kernel(by, at_ref, q_ref, o_ref, l_ref, m_ref, face_ref, mine_ref, other_ref, mine9_ref, other9_ref, out_ref):
    chunk, core = jnp.bitwise_and(at_ref[0] + by, 3), jnp.bitwise_and(at_ref[1], 1)
    q = q_ref[pl.ds(pl.multiple_of(chunk * CHUNK, CHUNK), CHUNK)]
    mine, other = [
        jnp.concatenate([four[...].reshape(4 * BLK, WIDE), last[...]], 0)
        for four, last in ((mine_ref, mine9_ref), (other_ref, other9_ref))
    ]
    k = jnp.concatenate([face_ref[0, pl.ds(0, BLK)], jnp.where(core == 0, mine, other)], 0)
    v = jnp.concatenate([face_ref[1, pl.ds(0, BLK)], jnp.where(core == 0, other, mine)], 0)
    for pair in range(2):
        k1, v1 = twice(k, pair), ones_beside(v, pair)
        sums, tops = [], []
        for qh in spread(q, pair):
            s = scores(qh, k1)
            m = jnp.max(s, axis=1, keepdims=True)
            sums.append(jnp.dot(jnp.exp2(s - m).astype(BF16), v1, preferred_element_type=F32))
            tops.append(m)
        cols = pl.ds(pair * 128, 128)
        o = select(sums[0][:, :128], sums[1][:, :128])
        l = select(sums[0][:, 128:], sums[1][:, 128:])
        m = select(*tops)
        before = m_ref[:, cols]
        top = jnp.maximum(m, before)
        a, b = jnp.exp2(before - top), jnp.exp2(m - top)
        out = (o * b + o_ref[:, cols] * a) / (l * b + l_ref[:, cols] * a)
        out_ref[:, cols] = out.astype(BF16)


def times(at_ref, att_ref, mine_ref, other_ref):
    first = jnp.bitwise_and(at_ref[1], 1) == 0
    return jnp.dot(
        att_ref[...], ordered(first, mine_ref[...], other_ref[...]), preferred_element_type=F32
    )


def project_kernel(at_ref, own_ref, w_own_ref, *refs):
    total = jnp.dot(own_ref[...], w_own_ref[...], preferred_element_type=F32)
    for i in range(3):
        total = total + times(at_ref, *refs[3 * i : 3 * i + 3])
    refs[9][...] = total.astype(BF16)


def body(queries, keys_values, out_weight):
    shards = lax.axis_size("ctx")
    heads = lax.axis_size("head")
    place = lax.axis_index("ctx")
    rank = lax.axis_index("head")
    at = jnp.stack([rank, place]).astype(jnp.int32)
    barrier = lax.optimization_barrier

    def swap(x, bits):
        return lax.ppermute(x, "ctx", [(i, i ^ bits) for i in range(shards)])

    def turn(x, by):
        return lax.ppermute(x, "head", [(i, (i + by) % heads) for i in range(heads)])

    panel, half = ((BLK, WIDE), BF16), ((BLK // 2, WIDE), BF16)
    levels, face, back = call(
        pyramid_kernel,
        "pyramid",
        [((2, 3840, WIDE), BF16), ((2, 2 * BLK, WIDE), BF16), ((2, BLK, WIDE), BF16)],
        (at, keys_values, queries),
    )
    turns = (2, 1, 3, 0)
    sibling = swap(face, 1)
    ends = [(i, i + 1) for i in range(1, shards - 1, 2)]
    back = lax.ppermute(back, "ctx", ends + [(b, a) for a, b in ends])

    def near(chunks, gate):
        return call(
            functools.partial(near_kernel, [turns[i] for i in chunks], shards),
            "near",
            [((CHUNK, WIDE), F32)] * (3 * len(chunks)),
            (at, queries, levels, sibling, back),
            (gate,),
        )

    def exchange(up, part, bit):
        return swap(up, 1 << bit), swap(part, 2 << bit), swap(part, 3 << bit)

    up5, part6 = call(start_kernel, "start", [panel, half], (at, face, sibling))
    got = exchange(up5, part6, 1)
    near0 = near((0,), up5)
    *got, near0[0] = barrier((*got, near0[0]))
    p6, up7, part8, w_half = call(
        middle_kernel,
        "middle",
        [panel, panel, half, ((128, 1024), BF16)],
        (at, up5, *got, out_weight),
    )
    p5 = got[0]
    got = exchange(up7, part8, 3)
    near1 = near((1,), up7)
    *got, near1[0] = barrier((*got, near1[0]))
    w2 = turn(w_half, 2)
    up9, held = call(last_kernel, "last", [panel, ((4, BLK, WIDE), BF16)], (at, up7, *got, p5, p6))
    p9 = swap(up9, 56)
    theirs = swap(held, 1)
    near23 = near((2, 3), up9)
    p9, near23[0] = barrier((p9, near23[0]))
    near2, near3 = near23[:3], near23[3:]
    theirs9 = swap(p9, 1)
    w2, source = barrier((w2, w_half))
    w_mine = [w2, turn(source, 1), turn(source, 3)]
    w_other = [swap(w, 1) for w in w_mine]
    atts = []
    for by, state in zip(turns, (near0, near1, near2, near3)):
        (att,) = call(
            functools.partial(far_kernel, by),
            "far",
            [((CHUNK, WIDE), BF16)],
            (at, queries, *state, sibling, held, theirs, p9, theirs9),
        )
        atts.append(turn(att, by) if by else att)
    pieces = list(zip(atts, w_mine, w_other))
    (out,) = call(
        project_kernel,
        "project",
        [((CHUNK, 1024), BF16)],
        (at, atts[3], out_weight, *pieces[2], *pieces[1], *pieces[0]),
    )
    return out


def solution(mesh):
    in_specs = (P("ctx", "head"), P(None, "ctx", "head"), P("head", None))
    out_specs = P(("ctx", "head"), None)
    return jax.shard_map(body, mesh=mesh, in_specs=in_specs, out_specs=out_specs, check_vma=False)
```

```python
import functools
import math

import jax
import jax.numpy as jnp
from jax import lax
from jax.experimental import pallas as pl
from jax.experimental.pallas import tpu as pltpu
from jax.sharding import PartitionSpec as P

HD = 64
BLK = 128
WIDE = 256
CHUNK = 512
SCALE = math.log2(math.e) / math.sqrt(HD)
ROOT = 1.0 / math.sqrt(2.0)
HIDE = -1e30
NT = (((1,), (1,)), ((), ()))
F32 = jnp.float32
BF16 = jnp.bfloat16

VMEM = pl.BlockSpec(memory_space=pltpu.VMEM)
SMEM = pl.BlockSpec(memory_space=pltpu.SMEM)


def call(kernel, name, outs, args, after=(), limit=16):
    n, late = len(args), len(after)
    return list(
        pl.pallas_call(
            lambda *refs: kernel(*refs[:n], *refs[n + late :]),
            out_shape=[jax.ShapeDtypeStruct(shape, dtype) for shape, dtype in outs],
            in_specs=[SMEM] + [VMEM] * (n - 1) + [pl.BlockSpec(memory_space=pl.ANY)] * late,
            out_specs=[VMEM] * len(outs),
            compiler_params=pltpu.CompilerParams(vmem_limit_bytes=limit * 2**20),
            name=name,
        )(*args, *after)
    )


def halve(rows):
    n = rows.shape[0]
    out = lax.broadcasted_iota(jnp.int32, (n // 2, n), 0)
    col = lax.broadcasted_iota(jnp.int32, (n // 2, n), 1)
    pairs = (col // 2 == out).astype(BF16)
    return (jnp.dot(pairs, rows, preferred_element_type=F32) * ROOT).astype(BF16)


def spread(q, pair):
    x = q[:, pair * 128 : pair * 128 + 128].astype(F32) * SCALE
    head = x.astype(BF16)
    rest = (x - head.astype(F32)).astype(BF16)
    low = lax.broadcasted_iota(jnp.int32, head.shape, 1) < HD
    zero = jnp.zeros_like(head)
    return [
        jnp.concatenate([jnp.where(keep, head, zero), jnp.where(keep, rest, zero)], 1)
        for keep in (low, jnp.logical_not(low))
    ]


def twice(k, pair):
    k = k[:, pair * 128 : pair * 128 + 128]
    return jnp.concatenate([k, k], 1)


def ones_beside(v, pair):
    v = v[:, pair * 128 : pair * 128 + 128]
    return jnp.concatenate([v, jnp.ones_like(v)], 1)


def scores(q, k):
    return lax.dot_general(q, k, NT, preferred_element_type=F32)


def select(x0, x1):
    low = lax.broadcasted_iota(jnp.int32, (x0.shape[0], 128), 1) < HD
    return jnp.where(low, x0, x1)


def pyramid_kernel(at_ref, kv_ref, q_ref, lev_ref, face_ref, back_ref):
    even = jnp.bitwise_and(at_ref[1], 1) == 0
    for side in range(2):
        for i in range(8):
            rows = kv_ref[side, pl.ds(i * 256, 256)]
            lev_ref[side, pl.ds(i * 256, 256)] = rows
            lev_ref[side, pl.ds(2048 + i * 128, 128)] = halve(rows)
        first, last = kv_ref[side, pl.ds(0, BLK)], kv_ref[side, pl.ds(2048 - BLK, BLK)]
        face_ref[side, pl.ds(BLK, BLK)] = jnp.where(even, last, first)
        back_ref[side] = jnp.where(even, first, last)
    for side in range(2):
        for i in range(4):
            lev_ref[side, pl.ds(3072 + i * 128, 128)] = halve(lev_ref[side, pl.ds(2048 + i * 256, 256)])
    for side in range(2):
        for i in range(2):
            lev_ref[side, pl.ds(3584 + i * 128, 128)] = halve(lev_ref[side, pl.ds(3072 + i * 256, 256)])
    for side in range(2):
        face_ref[side, pl.ds(0, BLK)] = halve(lev_ref[side, pl.ds(3584, 256)])


def bit_of(at_ref, bit):
    return jnp.bitwise_and(lax.shift_right_logical(at_ref[1], bit), 1) == 0


def ordered(low, mine, other):
    return jnp.concatenate([jnp.where(low, mine, other), jnp.where(low, other, mine)], 0)


def start_kernel(at_ref, mine_ref, other_ref, up_ref, half_ref):
    side = jnp.bitwise_and(at_ref[1], 1)
    up = ordered(
        bit_of(at_ref, 0), halve(mine_ref[side, pl.ds(0, BLK)]), halve(other_ref[side, pl.ds(0, BLK)])
    )
    up_ref[...] = up
    half_ref[...] = halve(up)


def climb(bit, at_ref, mine_ref, near_ref, same_ref, cross_ref):
    low = bit_of(at_ref, bit)
    own = ordered(low, halve(mine_ref[...]), halve(near_ref[...]))
    sibling = ordered(low, same_ref[...], cross_ref[...])
    return sibling, ordered(bit_of(at_ref, bit + 1), halve(own), halve(sibling))


def middle_kernel(at_ref, mine_ref, near_ref, same_ref, cross_ref, w_ref, sib_ref, up_ref, half_ref, w_half_ref):
    sib_ref[...], up = climb(1, at_ref, mine_ref, near_ref, same_ref, cross_ref)
    up_ref[...] = up
    half_ref[...] = halve(up)
    core = jnp.bitwise_and(at_ref[1], 1)
    w_half_ref[...] = w_ref[pl.ds(pl.multiple_of(core * 128, 128), 128)]


def last_kernel(at_ref, mine_ref, near_ref, same_ref, cross_ref, p5_ref, p6_ref, up_ref, held_ref):
    held_ref[0], held_ref[1], held_ref[2] = p5_ref[...], p6_ref[...], near_ref[...]
    held_ref[3], up_ref[...] = climb(3, at_ref, mine_ref, near_ref, same_ref, cross_ref)


def near_chunk(by, shards, at_ref, q_ref, lev_ref, face_ref, back_ref, o_ref, l_ref, m_ref):
    chunk, place = jnp.bitwise_and(at_ref[0] + by, 3), at_ref[1]
    even = jnp.bitwise_and(place, 1) == 0

    def panel(ref, side, start, rows=BLK):
        return ref[side, pl.ds(pl.multiple_of(start, BLK), rows)]
    for t in range(2):
        base = chunk * CHUNK + t * 256
        q = q_ref[pl.ds(pl.multiple_of(base, 256), 256)]
        parts = []
        for side in range(2):
            main = jnp.concatenate([
                panel(lev_ref, side, base, 256),
                panel(lev_ref, side, 2048 + chunk * 256 + (1 - t) * BLK),
                panel(lev_ref, side, 3072 + jnp.bitwise_xor(chunk, 1) * BLK)], 0)
            third = panel(lev_ref, side, 3584 + jnp.bitwise_xor(lax.shift_right_logical(chunk, 1), 1) * BLK)
            if t == 0:
                low = panel(lev_ref, side, jnp.maximum(base - BLK, 0))
                halo = jnp.where(even, back_ref[side], face_ref[side, pl.ds(BLK, BLK)])
                low = jnp.where(chunk == 0, halo, low)
                high = panel(lev_ref, side, base + 256)
            else:
                low = panel(lev_ref, side, base - BLK)
                high = panel(lev_ref, side, jnp.minimum(base + 256, 2048 - BLK))
                halo = jnp.where(even, face_ref[side, pl.ds(BLK, BLK)], back_ref[side])
                high = jnp.where(chunk == 3, halo, high)
            parts.append((main, jnp.concatenate([third, low], 0), jnp.concatenate([third, high], 0)))
        ks, vs = parts
        for pair in range(2):
            h0, h1 = spread(q, pair)
            qs = jnp.concatenate([h0[:128], h1[:128], h0[128:], h1[128:]], 0)
            k1, k2, k3 = [twice(k, pair) for k in ks]
            v1, v2, v3 = [ones_beside(v, pair) for v in vs]
            s1 = scores(qs, k1)
            s2 = scores(qs[:256], k2)
            s3 = scores(qs[256:], k3)
            if t == 0:
                bias = jnp.where((chunk == 0) & (place == 0), HIDE, 0.0)
                s2 = jnp.concatenate([s2[:, :128], s2[:, 128:] + bias], 1)
            else:
                bias = jnp.where((chunk == 3) & (place == shards - 1), HIDE, 0.0)
                s3 = jnp.concatenate([s3[:, :128], s3[:, 128:] + bias], 1)
            s23 = jnp.concatenate([s2, s3], 0)
            m = jnp.max(jnp.concatenate([s1, s23], 1), axis=1, keepdims=True)
            p1 = jnp.exp2(s1 - m).astype(BF16)
            p23 = jnp.exp2(s23 - m).astype(BF16)
            o = jnp.dot(p1, v1, preferred_element_type=F32)
            o = o + jnp.concatenate([jnp.dot(p23[:256], v2, preferred_element_type=F32),
                                     jnp.dot(p23[256:], v3, preferred_element_type=F32)], 0)
            for part in range(2):
                r = part * 256
                rows = pl.ds(t * 256 + part * 128, 128)
                cols = pl.ds(pair * 128, 128)
                o_ref[rows, cols] = select(o[r:r+128, :128], o[r+128:r+256, :128])
                l_ref[rows, cols] = select(o[r:r+128, 128:], o[r+128:r+256, 128:])
                m_ref[rows, cols] = select(m[r:r+128], m[r+128:r+256])


def near_kernel(turns, shards, *refs):
    for i, by in enumerate(turns):
        near_chunk(by, shards, *refs[:5], *refs[5 + 3 * i : 8 + 3 * i])


def far_kernel(by, at_ref, q_ref, o_ref, l_ref, m_ref, face_ref, mine_ref, other_ref, mine9_ref, other9_ref, out_ref):
    chunk, core = jnp.bitwise_and(at_ref[0] + by, 3), jnp.bitwise_and(at_ref[1], 1)
    q = q_ref[pl.ds(pl.multiple_of(chunk * CHUNK, CHUNK), CHUNK)]
    mine, other = [
        jnp.concatenate([four[...].reshape(4 * BLK, WIDE), last[...]], 0)
        for four, last in ((mine_ref, mine9_ref), (other_ref, other9_ref))
    ]
    k = jnp.concatenate([face_ref[0, pl.ds(0, BLK)], jnp.where(core == 0, mine, other)], 0)
    v = jnp.concatenate([face_ref[1, pl.ds(0, BLK)], jnp.where(core == 0, other, mine)], 0)
    for pair in range(2):
        k1, v1 = twice(k, pair), ones_beside(v, pair)
        sums, tops = [], []
        for qh in spread(q, pair):
            s = scores(qh, k1)
            m = jnp.max(s, axis=1, keepdims=True)
            sums.append(jnp.dot(jnp.exp2(s - m).astype(BF16), v1, preferred_element_type=F32))
            tops.append(m)
        cols = pl.ds(pair * 128, 128)
        o = select(sums[0][:, :128], sums[1][:, :128])
        l = select(sums[0][:, 128:], sums[1][:, 128:])
        m = select(*tops)
        before = m_ref[:, cols]
        top = jnp.maximum(m, before)
        a, b = jnp.exp2(before - top), jnp.exp2(m - top)
        out = (o * b + o_ref[:, cols] * a) / (l * b + l_ref[:, cols] * a)
        out_ref[:, cols] = out.astype(BF16)


def times(at_ref, att_ref, mine_ref, other_ref):
    first = jnp.bitwise_and(at_ref[1], 1) == 0
    return jnp.dot(
        att_ref[...], ordered(first, mine_ref[...], other_ref[...]), preferred_element_type=F32
    )


def project_kernel(at_ref, own_ref, w_own_ref, *refs):
    total = jnp.dot(own_ref[...], w_own_ref[...], preferred_element_type=F32)
    for i in range(3):
        total = total + times(at_ref, *refs[3 * i : 3 * i + 3])
    refs[9][...] = total.astype(BF16)


def body(queries, keys_values, out_weight):
    shards = lax.axis_size("ctx")
    heads = lax.axis_size("head")
    place = lax.axis_index("ctx")
    rank = lax.axis_index("head")
    at = jnp.stack([rank, place]).astype(jnp.int32)
    barrier = lax.optimization_barrier

    def swap(x, bits):
        return lax.ppermute(x, "ctx", [(i, i ^ bits) for i in range(shards)])

    def turn(x, by):
        return lax.ppermute(x, "head", [(i, (i + by) % heads) for i in range(heads)])

    panel, half = ((BLK, WIDE), BF16), ((BLK // 2, WIDE), BF16)
    levels, face, back = call(
        pyramid_kernel,
        "pyramid",
        [((2, 3840, WIDE), BF16), ((2, 2 * BLK, WIDE), BF16), ((2, BLK, WIDE), BF16)],
        (at, keys_values, queries),
    )
    turns = (2, 1, 3, 0)
    sibling = swap(face, 1)
    ends = [(i, i + 1) for i in range(1, shards - 1, 2)]
    back = lax.ppermute(back, "ctx", ends + [(b, a) for a, b in ends])

    def near(chunks, gate):
        return call(
            functools.partial(near_kernel, [turns[i] for i in chunks], shards),
            "near",
            [((CHUNK, WIDE), F32)] * (3 * len(chunks)),
            (at, queries, levels, sibling, back),
            (gate,),
        )

    def exchange(up, part, bit):
        return swap(up, 1 << bit), swap(part, 2 << bit), swap(part, 3 << bit)

    up5, part6 = call(start_kernel, "start", [panel, half], (at, face, sibling))
    got = exchange(up5, part6, 1)
    near0 = near((0,), up5)
    *got, near0[0] = barrier((*got, near0[0]))
    p6, up7, part8, w_half = call(
        middle_kernel,
        "middle",
        [panel, panel, half, ((128, 1024), BF16)],
        (at, up5, *got, out_weight),
    )
    p5 = got[0]
    got = exchange(up7, part8, 3)
    near1 = near((1,), up7)
    *got, near1[0] = barrier((*got, near1[0]))
    w2, w1 = turn(w_half, 2), turn(w_half, 1)
    up9, held = call(last_kernel, "last", [panel, ((4, BLK, WIDE), BF16)], (at, up7, *got, p5, p6))
    p9 = swap(up9, 56)
    theirs = swap(held, 1)
    near23 = near((2, 3), up9)
    p9, near23[0] = barrier((p9, near23[0]))
    near2, near3 = near23[:3], near23[3:]
    theirs9 = swap(p9, 1)
    w2, source = barrier((w2, w_half))
    w_mine = [w2, w1, turn(source, 3)]
    w_other = [swap(w, 1) for w in w_mine]
    atts = []
    for by, state in zip(turns, (near0, near1, near2, near3)):
        (att,) = call(
            functools.partial(far_kernel, by),
            "far",
            [((CHUNK, WIDE), BF16)],
            (at, queries, *state, sibling, held, theirs, p9, theirs9),
        )
        atts.append(turn(att, by) if by else att)
    pieces = list(zip(atts, w_mine, w_other))
    (out,) = call(
        project_kernel,
        "project",
        [((CHUNK, 1024), BF16)],
        (at, atts[3], out_weight, *pieces[2], *pieces[1], *pieces[0]),
    )
    return out


def solution(mesh):
    in_specs = (P("ctx", "head"), P(None, "ctx", "head"), P("head", None))
    out_specs = P(("ctx", "head"), None)
    return jax.shard_map(body, mesh=mesh, in_specs=in_specs, out_specs=out_specs, check_vma=False)
```

```python
import functools
import math

import jax
import jax.numpy as jnp
from jax import lax
from jax.experimental import pallas as pl
from jax.experimental.pallas import tpu as pltpu
from jax.sharding import PartitionSpec as P

HD = 64
BLK = 128
WIDE = 256
CHUNK = 512
SCALE = math.log2(math.e) / math.sqrt(HD)
ROOT = 1.0 / math.sqrt(2.0)
HIDE = -1e30
NT = (((1,), (1,)), ((), ()))
F32 = jnp.float32
BF16 = jnp.bfloat16

VMEM = pl.BlockSpec(memory_space=pltpu.VMEM)
SMEM = pl.BlockSpec(memory_space=pltpu.SMEM)


def call(kernel, name, outs, args, after=(), limit=16):
    n, late = len(args), len(after)
    return list(
        pl.pallas_call(
            lambda *refs: kernel(*refs[:n], *refs[n + late :]),
            out_shape=[jax.ShapeDtypeStruct(shape, dtype) for shape, dtype in outs],
            in_specs=[SMEM] + [VMEM] * (n - 1) + [pl.BlockSpec(memory_space=pl.ANY)] * late,
            out_specs=[VMEM] * len(outs),
            compiler_params=pltpu.CompilerParams(vmem_limit_bytes=limit * 2**20),
            name=name,
        )(*args, *after)
    )


def halve(rows):
    n = rows.shape[0]
    out = lax.broadcasted_iota(jnp.int32, (n // 2, n), 0)
    col = lax.broadcasted_iota(jnp.int32, (n // 2, n), 1)
    pairs = (col // 2 == out).astype(BF16)
    return (jnp.dot(pairs, rows, preferred_element_type=F32) * ROOT).astype(BF16)


def spread(q, pair):
    x = q[:, pair * 128 : pair * 128 + 128].astype(F32) * SCALE
    head = x.astype(BF16)
    rest = (x - head.astype(F32)).astype(BF16)
    low = lax.broadcasted_iota(jnp.int32, head.shape, 1) < HD
    zero = jnp.zeros_like(head)
    return [
        jnp.concatenate([jnp.where(keep, head, zero), jnp.where(keep, rest, zero)], 1)
        for keep in (low, jnp.logical_not(low))
    ]


def twice(k, pair):
    k = k[:, pair * 128 : pair * 128 + 128]
    return jnp.concatenate([k, k], 1)


def ones_beside(v, pair):
    v = v[:, pair * 128 : pair * 128 + 128]
    return jnp.concatenate([v, jnp.ones_like(v)], 1)


def scores(q, k):
    return lax.dot_general(q, k, NT, preferred_element_type=F32)


def select(x0, x1):
    low = lax.broadcasted_iota(jnp.int32, (x0.shape[0], 128), 1) < HD
    return jnp.where(low, x0, x1)


def pyramid_kernel(at_ref, kv_ref, q_ref, lev_ref, face_ref, back_ref):
    even = jnp.bitwise_and(at_ref[1], 1) == 0
    for side in range(2):
        for i in range(8):
            rows = kv_ref[side, pl.ds(i * 256, 256)]
            lev_ref[side, pl.ds(i * 256, 256)] = rows
            lev_ref[side, pl.ds(2048 + i * 128, 128)] = halve(rows)
        first, last = kv_ref[side, pl.ds(0, BLK)], kv_ref[side, pl.ds(2048 - BLK, BLK)]
        face_ref[side, pl.ds(BLK, BLK)] = jnp.where(even, last, first)
        back_ref[side] = jnp.where(even, first, last)
    for side in range(2):
        for i in range(4):
            lev_ref[side, pl.ds(3072 + i * 128, 128)] = halve(lev_ref[side, pl.ds(2048 + i * 256, 256)])
    for side in range(2):
        for i in range(2):
            lev_ref[side, pl.ds(3584 + i * 128, 128)] = halve(lev_ref[side, pl.ds(3072 + i * 256, 256)])
    for side in range(2):
        face_ref[side, pl.ds(0, BLK)] = halve(lev_ref[side, pl.ds(3584, 256)])


def bit_of(at_ref, bit):
    return jnp.bitwise_and(lax.shift_right_logical(at_ref[1], bit), 1) == 0


def ordered(low, mine, other):
    return jnp.concatenate([jnp.where(low, mine, other), jnp.where(low, other, mine)], 0)


def start_kernel(at_ref, mine_ref, other_ref, up_ref, half_ref):
    side = jnp.bitwise_and(at_ref[1], 1)
    up = ordered(
        bit_of(at_ref, 0), halve(mine_ref[side, pl.ds(0, BLK)]), halve(other_ref[side, pl.ds(0, BLK)])
    )
    up_ref[...] = up
    half_ref[...] = halve(up)


def climb(bit, at_ref, mine_ref, near_ref, same_ref, cross_ref):
    low = bit_of(at_ref, bit)
    own = ordered(low, halve(mine_ref[...]), halve(near_ref[...]))
    sibling = ordered(low, same_ref[...], cross_ref[...])
    return sibling, ordered(bit_of(at_ref, bit + 1), halve(own), halve(sibling))


def middle_kernel(at_ref, mine_ref, near_ref, same_ref, cross_ref, w_ref, sib_ref, up_ref, half_ref, w_half_ref):
    sib_ref[...], up = climb(1, at_ref, mine_ref, near_ref, same_ref, cross_ref)
    up_ref[...] = up
    half_ref[...] = halve(up)
    core = jnp.bitwise_and(at_ref[1], 1)
    w_half_ref[...] = w_ref[pl.ds(pl.multiple_of(core * 128, 128), 128)]


def last_kernel(at_ref, mine_ref, near_ref, same_ref, cross_ref, p5_ref, p6_ref, w_ref, up_ref, held_ref, w_out_ref):
    w_out_ref[...] = w_ref[...]
    held_ref[0], held_ref[1], held_ref[2] = p5_ref[...], p6_ref[...], near_ref[...]
    held_ref[3], up_ref[...] = climb(3, at_ref, mine_ref, near_ref, same_ref, cross_ref)


def near_chunk(by, shards, at_ref, q_ref, lev_ref, face_ref, back_ref, o_ref, l_ref, m_ref):
    chunk, place = jnp.bitwise_and(at_ref[0] + by, 3), at_ref[1]
    even = jnp.bitwise_and(place, 1) == 0

    def panel(ref, side, start, rows=BLK):
        return ref[side, pl.ds(pl.multiple_of(start, BLK), rows)]
    for t in range(2):
        base = chunk * CHUNK + t * 256
        q = q_ref[pl.ds(pl.multiple_of(base, 256), 256)]
        parts = []
        for side in range(2):
            main = jnp.concatenate([
                panel(lev_ref, side, base, 256),
                panel(lev_ref, side, 2048 + chunk * 256 + (1 - t) * BLK),
                panel(lev_ref, side, 3072 + jnp.bitwise_xor(chunk, 1) * BLK)], 0)
            third = panel(lev_ref, side, 3584 + jnp.bitwise_xor(lax.shift_right_logical(chunk, 1), 1) * BLK)
            if t == 0:
                low = panel(lev_ref, side, jnp.maximum(base - BLK, 0))
                halo = jnp.where(even, back_ref[side], face_ref[side, pl.ds(BLK, BLK)])
                low = jnp.where(chunk == 0, halo, low)
                high = panel(lev_ref, side, base + 256)
            else:
                low = panel(lev_ref, side, base - BLK)
                high = panel(lev_ref, side, jnp.minimum(base + 256, 2048 - BLK))
                halo = jnp.where(even, face_ref[side, pl.ds(BLK, BLK)], back_ref[side])
                high = jnp.where(chunk == 3, halo, high)
            parts.append((main, jnp.concatenate([third, low], 0), jnp.concatenate([third, high], 0)))
        ks, vs = parts
        for pair in range(2):
            h0, h1 = spread(q, pair)
            qs = jnp.concatenate([h0[:128], h1[:128], h0[128:], h1[128:]], 0)
            k1, k2, k3 = [twice(k, pair) for k in ks]
            v1, v2, v3 = [ones_beside(v, pair) for v in vs]
            s1 = scores(qs, k1)
            s2 = scores(qs[:256], k2)
            s3 = scores(qs[256:], k3)
            if t == 0:
                bias = jnp.where((chunk == 0) & (place == 0), HIDE, 0.0)
                s2 = jnp.concatenate([s2[:, :128], s2[:, 128:] + bias], 1)
            else:
                bias = jnp.where((chunk == 3) & (place == shards - 1), HIDE, 0.0)
                s3 = jnp.concatenate([s3[:, :128], s3[:, 128:] + bias], 1)
            s23 = jnp.concatenate([s2, s3], 0)
            m = jnp.max(jnp.concatenate([s1, s23], 1), axis=1, keepdims=True)
            p1 = jnp.exp2(s1 - m).astype(BF16)
            p23 = jnp.exp2(s23 - m).astype(BF16)
            o = jnp.dot(p1, v1, preferred_element_type=F32)
            o = o + jnp.concatenate([jnp.dot(p23[:256], v2, preferred_element_type=F32),
                                     jnp.dot(p23[256:], v3, preferred_element_type=F32)], 0)
            for part in range(2):
                r = part * 256
                rows = pl.ds(t * 256 + part * 128, 128)
                cols = pl.ds(pair * 128, 128)
                o_ref[rows, cols] = select(o[r:r+128, :128], o[r+128:r+256, :128])
                l_ref[rows, cols] = select(o[r:r+128, 128:], o[r+128:r+256, 128:])
                m_ref[rows, cols] = select(m[r:r+128], m[r+128:r+256])


def near_kernel(turns, shards, *refs):
    for i, by in enumerate(turns):
        near_chunk(by, shards, *refs[:5], *refs[5 + 3 * i : 8 + 3 * i])


def far_kernel(by, at_ref, q_ref, o_ref, l_ref, m_ref, face_ref, mine_ref, other_ref, mine9_ref, other9_ref, out_ref):
    chunk, core = jnp.bitwise_and(at_ref[0] + by, 3), jnp.bitwise_and(at_ref[1], 1)
    q = q_ref[pl.ds(pl.multiple_of(chunk * CHUNK, CHUNK), CHUNK)]
    mine, other = [
        jnp.concatenate([four[...].reshape(4 * BLK, WIDE), last[...]], 0)
        for four, last in ((mine_ref, mine9_ref), (other_ref, other9_ref))
    ]
    k = jnp.concatenate([face_ref[0, pl.ds(0, BLK)], jnp.where(core == 0, mine, other)], 0)
    v = jnp.concatenate([face_ref[1, pl.ds(0, BLK)], jnp.where(core == 0, other, mine)], 0)
    for pair in range(2):
        k1, v1 = twice(k, pair), ones_beside(v, pair)
        sums, tops = [], []
        for qh in spread(q, pair):
            s = scores(qh, k1)
            m = jnp.max(s, axis=1, keepdims=True)
            sums.append(jnp.dot(jnp.exp2(s - m).astype(BF16), v1, preferred_element_type=F32))
            tops.append(m)
        cols = pl.ds(pair * 128, 128)
        o = select(sums[0][:, :128], sums[1][:, :128])
        l = select(sums[0][:, 128:], sums[1][:, 128:])
        m = select(*tops)
        before = m_ref[:, cols]
        top = jnp.maximum(m, before)
        a, b = jnp.exp2(before - top), jnp.exp2(m - top)
        out = (o * b + o_ref[:, cols] * a) / (l * b + l_ref[:, cols] * a)
        out_ref[:, cols] = out.astype(BF16)


def pack_kernel(at_ref, *refs):
    for i in range(3):
        refs[3][i] = refs[i][...]


def times(at_ref, att_ref, mine, other):
    first = jnp.bitwise_and(at_ref[1], 1) == 0
    return jnp.dot(att_ref[...], ordered(first, mine, other), preferred_element_type=F32)


def project_kernel(at_ref, own_ref, w_own_ref, mine_ref, other_ref, *refs):
    total = jnp.dot(own_ref[...], w_own_ref[...], preferred_element_type=F32)
    for i in range(3):
        total = total + times(at_ref, refs[i], mine_ref[i], other_ref[i])
    refs[3][...] = total.astype(BF16)


def body(queries, keys_values, out_weight):
    shards = lax.axis_size("ctx")
    heads = lax.axis_size("head")
    place = lax.axis_index("ctx")
    rank = lax.axis_index("head")
    at = jnp.stack([rank, place]).astype(jnp.int32)
    barrier = lax.optimization_barrier

    def swap(x, bits):
        return lax.ppermute(x, "ctx", [(i, i ^ bits) for i in range(shards)])

    def turn(x, by):
        return lax.ppermute(x, "head", [(i, (i + by) % heads) for i in range(heads)])

    panel, half = ((BLK, WIDE), BF16), ((BLK // 2, WIDE), BF16)
    levels, face, back = call(
        pyramid_kernel,
        "pyramid",
        [((2, 3840, WIDE), BF16), ((2, 2 * BLK, WIDE), BF16), ((2, BLK, WIDE), BF16)],
        (at, keys_values, queries),
    )
    turns = (2, 1, 3, 0)
    sibling = swap(face, 1)
    ends = [(i, i + 1) for i in range(1, shards - 1, 2)]
    back = lax.ppermute(back, "ctx", ends + [(b, a) for a, b in ends])

    def near(chunks, gate):
        return call(
            functools.partial(near_kernel, [turns[i] for i in chunks], shards),
            "near",
            [((CHUNK, WIDE), F32)] * (3 * len(chunks)),
            (at, queries, levels, sibling, back),
            (gate,),
        )

    def exchange(up, part, bit):
        return swap(up, 1 << bit), swap(part, 2 << bit), swap(part, 3 << bit)

    up5, part6 = call(start_kernel, "start", [panel, half], (at, face, sibling))
    got = exchange(up5, part6, 1)
    near0 = near((0,), up5)
    *got, near0[0] = barrier((*got, near0[0]))
    p6, up7, part8, w_half = call(
        middle_kernel,
        "middle",
        [panel, panel, half, ((128, 1024), BF16)],
        (at, up5, *got, out_weight),
    )
    p5 = got[0]
    got = exchange(up7, part8, 3)
    near1 = near((1,), up7)
    *got, near1[0] = barrier((*got, near1[0]))
    w2 = turn(w_half, 2)
    up9, held, w_late = call(
        last_kernel,
        "last",
        [panel, ((4, BLK, WIDE), BF16), ((128, 1024), BF16)],
        (at, up7, *got, p5, p6, w_half),
    )
    p9 = swap(up9, 56)
    theirs = swap(held, 1)
    near23 = near((2, 3), up9)
    p9, near23[0] = barrier((p9, near23[0]))
    near2, near3 = near23[:3], near23[3:]
    theirs9 = swap(p9, 1)
    w_mine = [w2, turn(w_half, 1), turn(w_late, 3)]
    (packed,) = call(pack_kernel, "pack", [((3, 128, 1024), BF16)], (at, *w_mine), (near2[0],))
    packed_other = swap(packed, 1)
    atts = []
    for by, state in zip(turns, (near0, near1, near2, near3)):
        (att,) = call(
            functools.partial(far_kernel, by),
            "far",
            [((CHUNK, WIDE), BF16)],
            (at, queries, *state, sibling, held, theirs, p9, theirs9),
        )
        atts.append(turn(att, by) if by else att)
    (out,) = call(
        project_kernel,
        "project",
        [((CHUNK, 1024), BF16)],
        (at, atts[3], out_weight, packed, packed_other, *atts[:3]),
    )
    return out


def solution(mesh):
    in_specs = (P("ctx", "head"), P(None, "ctx", "head"), P("head", None))
    out_specs = P(("ctx", "head"), None)
    return jax.shard_map(body, mesh=mesh, in_specs=in_specs, out_specs=out_specs, check_vma=False)
```

```python
import functools
import math

import jax
import jax.numpy as jnp
from jax import lax
from jax.experimental import pallas as pl
from jax.experimental.pallas import tpu as pltpu
from jax.sharding import PartitionSpec as P

HD = 64
BLK = 128
WIDE = 256
CHUNK = 512
SCALE = math.log2(math.e) / math.sqrt(HD)
ROOT = 1.0 / math.sqrt(2.0)
HIDE = -1e30
NT = (((1,), (1,)), ((), ()))
F32 = jnp.float32
BF16 = jnp.bfloat16

VMEM = pl.BlockSpec(memory_space=pltpu.VMEM)
SMEM = pl.BlockSpec(memory_space=pltpu.SMEM)


def call(kernel, name, outs, args, after=(), limit=16):
    n, late = len(args), len(after)
    return list(
        pl.pallas_call(
            lambda *refs: kernel(*refs[:n], *refs[n + late :]),
            out_shape=[jax.ShapeDtypeStruct(shape, dtype) for shape, dtype in outs],
            in_specs=[SMEM] + [VMEM] * (n - 1) + [pl.BlockSpec(memory_space=pl.ANY)] * late,
            out_specs=[VMEM] * len(outs),
            compiler_params=pltpu.CompilerParams(vmem_limit_bytes=limit * 2**20),
            name=name,
        )(*args, *after)
    )


def halve(rows):
    n = rows.shape[0]
    out = lax.broadcasted_iota(jnp.int32, (n // 2, n), 0)
    col = lax.broadcasted_iota(jnp.int32, (n // 2, n), 1)
    pairs = (col // 2 == out).astype(BF16)
    return (jnp.dot(pairs, rows, preferred_element_type=F32) * ROOT).astype(BF16)


def spread(q, pair):
    x = q[:, pair * 128 : pair * 128 + 128].astype(F32) * SCALE
    head = x.astype(BF16)
    rest = (x - head.astype(F32)).astype(BF16)
    low = lax.broadcasted_iota(jnp.int32, head.shape, 1) < HD
    zero = jnp.zeros_like(head)
    return [
        jnp.concatenate([jnp.where(keep, head, zero), jnp.where(keep, rest, zero)], 1)
        for keep in (low, jnp.logical_not(low))
    ]


def twice(k, pair):
    k = k[:, pair * 128 : pair * 128 + 128]
    return jnp.concatenate([k, k], 1)


def ones_beside(v, pair):
    v = v[:, pair * 128 : pair * 128 + 128]
    return jnp.concatenate([v, jnp.ones_like(v)], 1)


def scores(q, k):
    return lax.dot_general(q, k, NT, preferred_element_type=F32)


def select(x0, x1):
    low = lax.broadcasted_iota(jnp.int32, (x0.shape[0], 128), 1) < HD
    return jnp.where(low, x0, x1)


def pyramid_kernel(at_ref, kv_ref, q_ref, lev_ref, face_ref, back_ref):
    even = jnp.bitwise_and(at_ref[1], 1) == 0
    for side in range(2):
        for i in range(8):
            rows = kv_ref[side, pl.ds(i * 256, 256)]
            lev_ref[side, pl.ds(i * 256, 256)] = rows
            lev_ref[side, pl.ds(2048 + i * 128, 128)] = halve(rows)
        first, last = kv_ref[side, pl.ds(0, BLK)], kv_ref[side, pl.ds(2048 - BLK, BLK)]
        face_ref[side, pl.ds(BLK, BLK)] = jnp.where(even, last, first)
        back_ref[side] = jnp.where(even, first, last)
    for side in range(2):
        for i in range(4):
            lev_ref[side, pl.ds(3072 + i * 128, 128)] = halve(lev_ref[side, pl.ds(2048 + i * 256, 256)])
    for side in range(2):
        for i in range(2):
            lev_ref[side, pl.ds(3584 + i * 128, 128)] = halve(lev_ref[side, pl.ds(3072 + i * 256, 256)])
    for side in range(2):
        face_ref[side, pl.ds(0, BLK)] = halve(lev_ref[side, pl.ds(3584, 256)])


def bit_of(at_ref, bit):
    return jnp.bitwise_and(lax.shift_right_logical(at_ref[1], bit), 1) == 0


def ordered(low, mine, other):
    return jnp.concatenate([jnp.where(low, mine, other), jnp.where(low, other, mine)], 0)


def start_kernel(at_ref, mine_ref, other_ref, up_ref, half_ref):
    side = jnp.bitwise_and(at_ref[1], 1)
    up = ordered(
        bit_of(at_ref, 0), halve(mine_ref[side, pl.ds(0, BLK)]), halve(other_ref[side, pl.ds(0, BLK)])
    )
    up_ref[...] = up
    half_ref[...] = halve(up)


def climb(bit, at_ref, mine_ref, near_ref, same_ref, cross_ref):
    low = bit_of(at_ref, bit)
    own = ordered(low, halve(mine_ref[...]), halve(near_ref[...]))
    sibling = ordered(low, same_ref[...], cross_ref[...])
    return sibling, ordered(bit_of(at_ref, bit + 1), halve(own), halve(sibling))


def middle_kernel(at_ref, mine_ref, near_ref, same_ref, cross_ref, w_ref, sib_ref, up_ref, half_ref, w_half_ref):
    sib_ref[...], up = climb(1, at_ref, mine_ref, near_ref, same_ref, cross_ref)
    up_ref[...] = up
    half_ref[...] = halve(up)
    core = jnp.bitwise_and(at_ref[1], 1)
    w_half_ref[...] = w_ref[pl.ds(pl.multiple_of(core * 128, 128), 128)]


def last_kernel(at_ref, mine_ref, near_ref, same_ref, cross_ref, p5_ref, p6_ref, w_ref, up_ref, held_ref, w_out_ref):
    w_out_ref[...] = w_ref[...]
    held_ref[0], held_ref[1], held_ref[2] = p5_ref[...], p6_ref[...], near_ref[...]
    held_ref[3], up_ref[...] = climb(3, at_ref, mine_ref, near_ref, same_ref, cross_ref)


def near_chunk(by, shards, at_ref, q_ref, lev_ref, face_ref, back_ref, o_ref, l_ref, m_ref):
    chunk, place = jnp.bitwise_and(at_ref[0] + by, 3), at_ref[1]
    even = jnp.bitwise_and(place, 1) == 0

    def panel(ref, side, start, rows=BLK):
        return ref[side, pl.ds(pl.multiple_of(start, BLK), rows)]
    for t in range(2):
        base = chunk * CHUNK + t * 256
        q = q_ref[pl.ds(pl.multiple_of(base, 256), 256)]
        parts = []
        for side in range(2):
            main = jnp.concatenate([
                panel(lev_ref, side, base, 256),
                panel(lev_ref, side, 2048 + chunk * 256 + (1 - t) * BLK),
                panel(lev_ref, side, 3072 + jnp.bitwise_xor(chunk, 1) * BLK)], 0)
            third = panel(lev_ref, side, 3584 + jnp.bitwise_xor(lax.shift_right_logical(chunk, 1), 1) * BLK)
            if t == 0:
                low = panel(lev_ref, side, jnp.maximum(base - BLK, 0))
                halo = jnp.where(even, back_ref[side], face_ref[side, pl.ds(BLK, BLK)])
                low = jnp.where(chunk == 0, halo, low)
                high = panel(lev_ref, side, base + 256)
            else:
                low = panel(lev_ref, side, base - BLK)
                high = panel(lev_ref, side, jnp.minimum(base + 256, 2048 - BLK))
                halo = jnp.where(even, face_ref[side, pl.ds(BLK, BLK)], back_ref[side])
                high = jnp.where(chunk == 3, halo, high)
            parts.append((main, jnp.concatenate([third, low], 0), jnp.concatenate([third, high], 0)))
        ks, vs = parts
        for pair in range(2):
            h0, h1 = spread(q, pair)
            qs = jnp.concatenate([h0[:128], h1[:128], h0[128:], h1[128:]], 0)
            k1, k2, k3 = [twice(k, pair) for k in ks]
            v1, v2, v3 = [ones_beside(v, pair) for v in vs]
            s1 = scores(qs, k1)
            s2 = scores(qs[:256], k2)
            s3 = scores(qs[256:], k3)
            if t == 0:
                bias = jnp.where((chunk == 0) & (place == 0), HIDE, 0.0)
                s2 = jnp.concatenate([s2[:, :128], s2[:, 128:] + bias], 1)
            else:
                bias = jnp.where((chunk == 3) & (place == shards - 1), HIDE, 0.0)
                s3 = jnp.concatenate([s3[:, :128], s3[:, 128:] + bias], 1)
            s23 = jnp.concatenate([s2, s3], 0)
            m = jnp.max(jnp.concatenate([s1, s23], 1), axis=1, keepdims=True)
            p1 = jnp.exp2(s1 - m).astype(BF16)
            p23 = jnp.exp2(s23 - m).astype(BF16)
            o = jnp.dot(p1, v1, preferred_element_type=F32)
            o = o + jnp.concatenate([jnp.dot(p23[:256], v2, preferred_element_type=F32),
                                     jnp.dot(p23[256:], v3, preferred_element_type=F32)], 0)
            for part in range(2):
                r = part * 256
                rows = pl.ds(t * 256 + part * 128, 128)
                cols = pl.ds(pair * 128, 128)
                o_ref[rows, cols] = select(o[r:r+128, :128], o[r+128:r+256, :128])
                l_ref[rows, cols] = select(o[r:r+128, 128:], o[r+128:r+256, 128:])
                m_ref[rows, cols] = select(m[r:r+128], m[r+128:r+256])


def near_kernel(turns, shards, *refs):
    for i, by in enumerate(turns):
        near_chunk(by, shards, *refs[:5], *refs[5 + 3 * i : 8 + 3 * i])


def far_kernel(by, at_ref, q_ref, o_ref, l_ref, m_ref, face_ref, mine_ref, other_ref, mine9_ref, other9_ref, out_ref):
    chunk, core = jnp.bitwise_and(at_ref[0] + by, 3), jnp.bitwise_and(at_ref[1], 1)
    q = q_ref[pl.ds(pl.multiple_of(chunk * CHUNK, CHUNK), CHUNK)]
    mine, other = [
        jnp.concatenate([four[...].reshape(4 * BLK, WIDE), last[...]], 0)
        for four, last in ((mine_ref, mine9_ref), (other_ref, other9_ref))
    ]
    k = jnp.concatenate([face_ref[0, pl.ds(0, BLK)], jnp.where(core == 0, mine, other)], 0)
    v = jnp.concatenate([face_ref[1, pl.ds(0, BLK)], jnp.where(core == 0, other, mine)], 0)
    for pair in range(2):
        k1, v1 = twice(k, pair), ones_beside(v, pair)
        sums, tops = [], []
        for qh in spread(q, pair):
            s = scores(qh, k1)
            m = jnp.max(s, axis=1, keepdims=True)
            sums.append(jnp.dot(jnp.exp2(s - m).astype(BF16), v1, preferred_element_type=F32))
            tops.append(m)
        cols = pl.ds(pair * 128, 128)
        o = select(sums[0][:, :128], sums[1][:, :128])
        l = select(sums[0][:, 128:], sums[1][:, 128:])
        m = select(*tops)
        before = m_ref[:, cols]
        top = jnp.maximum(m, before)
        a, b = jnp.exp2(before - top), jnp.exp2(m - top)
        out = (o * b + o_ref[:, cols] * a) / (l * b + l_ref[:, cols] * a)
        out_ref[:, cols] = out.astype(BF16)


def pack_kernel(at_ref, *refs):
    for i in range(3):
        refs[3][i] = refs[i][...]


def times(at_ref, att_ref, mine, other):
    first = jnp.bitwise_and(at_ref[1], 1) == 0
    return jnp.dot(att_ref[...], ordered(first, mine, other), preferred_element_type=F32)


def project_kernel(at_ref, own_ref, w_own_ref, mine_ref, other_ref, *refs):
    total = jnp.dot(own_ref[...], w_own_ref[...], preferred_element_type=F32)
    for i in range(3):
        total = total + times(at_ref, refs[i], mine_ref[i], other_ref[i])
    refs[3][...] = total.astype(BF16)


def body(queries, keys_values, out_weight):
    shards = lax.axis_size("ctx")
    heads = lax.axis_size("head")
    place = lax.axis_index("ctx")
    rank = lax.axis_index("head")
    at = jnp.stack([rank, place]).astype(jnp.int32)
    barrier = lax.optimization_barrier

    def swap(x, bits):
        return lax.ppermute(x, "ctx", [(i, i ^ bits) for i in range(shards)])

    def turn(x, by):
        return lax.ppermute(x, "head", [(i, (i + by) % heads) for i in range(heads)])

    panel, half = ((BLK, WIDE), BF16), ((BLK // 2, WIDE), BF16)
    levels, face, back = call(
        pyramid_kernel,
        "pyramid",
        [((2, 3840, WIDE), BF16), ((2, 2 * BLK, WIDE), BF16), ((2, BLK, WIDE), BF16)],
        (at, keys_values, queries),
    )
    turns = (3, 1, 2, 0)
    sibling = swap(face, 1)
    ends = [(i, i + 1) for i in range(1, shards - 1, 2)]
    back = lax.ppermute(back, "ctx", ends + [(b, a) for a, b in ends])

    def near(chunks, gate):
        return call(
            functools.partial(near_kernel, [turns[i] for i in chunks], shards),
            "near",
            [((CHUNK, WIDE), F32)] * (3 * len(chunks)),
            (at, queries, levels, sibling, back),
            (gate,),
        )

    def exchange(up, part, bit):
        return swap(up, 1 << bit), swap(part, 2 << bit), swap(part, 3 << bit)

    up5, part6 = call(start_kernel, "start", [panel, half], (at, face, sibling))
    got = exchange(up5, part6, 1)
    near0 = near((0,), up5)
    *got, near0[0] = barrier((*got, near0[0]))
    p6, up7, part8, w_half = call(
        middle_kernel,
        "middle",
        [panel, panel, half, ((128, 1024), BF16)],
        (at, up5, *got, out_weight),
    )
    p5 = got[0]
    got = exchange(up7, part8, 3)
    near1 = near((1,), up7)
    *got, near1[0] = barrier((*got, near1[0]))
    w2 = turn(w_half, 2)
    up9, held, w_late = call(
        last_kernel,
        "last",
        [panel, ((4, BLK, WIDE), BF16), ((128, 1024), BF16)],
        (at, up7, *got, p5, p6, w_half),
    )
    p9 = swap(up9, 56)
    theirs = swap(held, 1)
    near23 = near((2, 3), up9)
    p9, near23[0] = barrier((p9, near23[0]))
    near2, near3 = near23[:3], near23[3:]
    theirs9 = swap(p9, 1)
    w_mine = [turn(w_late, 3), turn(w_half, 1), w2]
    (packed,) = call(pack_kernel, "pack", [((3, 128, 1024), BF16)], (at, *w_mine), (near2[0],))
    packed_other = swap(packed, 1)
    atts = []
    for by, state in zip(turns, (near0, near1, near2, near3)):
        (att,) = call(
            functools.partial(far_kernel, by),
            "far",
            [((CHUNK, WIDE), BF16)],
            (at, queries, *state, sibling, held, theirs, p9, theirs9),
        )
        atts.append(turn(att, by) if by else att)
    (out,) = call(
        project_kernel,
        "project",
        [((CHUNK, 1024), BF16)],
        (at, atts[3], out_weight, packed, packed_other, *atts[:3]),
    )
    return out


def solution(mesh):
    in_specs = (P("ctx", "head"), P(None, "ctx", "head"), P("head", None))
    out_specs = P(("ctx", "head"), None)
    return jax.shard_map(body, mesh=mesh, in_specs=in_specs, out_specs=out_specs, check_vma=False)
```

```python
import functools
import math

import jax
import jax.numpy as jnp
from jax import lax
from jax.experimental import pallas as pl
from jax.experimental.pallas import tpu as pltpu
from jax.sharding import PartitionSpec as P

HD = 64
BLK = 128
WIDE = 256
CHUNK = 512
SCALE = math.log2(math.e) / math.sqrt(HD)
ROOT = 1.0 / math.sqrt(2.0)
HIDE = -1e30
NT = (((1,), (1,)), ((), ()))
F32 = jnp.float32
BF16 = jnp.bfloat16

VMEM = pl.BlockSpec(memory_space=pltpu.VMEM)
SMEM = pl.BlockSpec(memory_space=pltpu.SMEM)


def call(kernel, name, outs, args, after=(), limit=16):
    n, late = len(args), len(after)
    return list(
        pl.pallas_call(
            lambda *refs: kernel(*refs[:n], *refs[n + late :]),
            out_shape=[jax.ShapeDtypeStruct(shape, dtype) for shape, dtype in outs],
            in_specs=[SMEM] + [VMEM] * (n - 1) + [pl.BlockSpec(memory_space=pl.ANY)] * late,
            out_specs=[VMEM] * len(outs),
            compiler_params=pltpu.CompilerParams(vmem_limit_bytes=limit * 2**20),
            name=name,
        )(*args, *after)
    )


def halve(rows):
    n = rows.shape[0]
    out = lax.broadcasted_iota(jnp.int32, (n // 2, n), 0)
    col = lax.broadcasted_iota(jnp.int32, (n // 2, n), 1)
    pairs = (col // 2 == out).astype(BF16)
    return (jnp.dot(pairs, rows, preferred_element_type=F32) * ROOT).astype(BF16)


def spread(q, pair):
    x = q[:, pair * 128 : pair * 128 + 128].astype(F32) * SCALE
    head = x.astype(BF16)
    rest = (x - head.astype(F32)).astype(BF16)
    low = lax.broadcasted_iota(jnp.int32, head.shape, 1) < HD
    zero = jnp.zeros_like(head)
    return [
        jnp.concatenate([jnp.where(keep, head, zero), jnp.where(keep, rest, zero)], 1)
        for keep in (low, jnp.logical_not(low))
    ]


def twice(k, pair):
    k = k[:, pair * 128 : pair * 128 + 128]
    return jnp.concatenate([k, k], 1)


def ones_beside(v, pair):
    v = v[:, pair * 128 : pair * 128 + 128]
    return jnp.concatenate([v, jnp.ones_like(v)], 1)


def scores(q, k):
    return lax.dot_general(q, k, NT, preferred_element_type=F32)


def select(x0, x1):
    low = lax.broadcasted_iota(jnp.int32, (x0.shape[0], 128), 1) < HD
    return jnp.where(low, x0, x1)


def pyramid_kernel(at_ref, kv_ref, q_ref, lev_ref, face_ref, back_ref):
    even = jnp.bitwise_and(at_ref[1], 1) == 0
    for side in range(2):
        for i in range(8):
            rows = kv_ref[side, pl.ds(i * 256, 256)]
            lev_ref[side, pl.ds(i * 256, 256)] = rows
            lev_ref[side, pl.ds(2048 + i * 128, 128)] = halve(rows)
        first, last = kv_ref[side, pl.ds(0, BLK)], kv_ref[side, pl.ds(2048 - BLK, BLK)]
        face_ref[side, pl.ds(BLK, BLK)] = jnp.where(even, last, first)
        back_ref[side] = jnp.where(even, first, last)
    for side in range(2):
        for i in range(4):
            lev_ref[side, pl.ds(3072 + i * 128, 128)] = halve(lev_ref[side, pl.ds(2048 + i * 256, 256)])
    for side in range(2):
        for i in range(2):
            lev_ref[side, pl.ds(3584 + i * 128, 128)] = halve(lev_ref[side, pl.ds(3072 + i * 256, 256)])
    for side in range(2):
        face_ref[side, pl.ds(0, BLK)] = halve(lev_ref[side, pl.ds(3584, 256)])


def bit_of(at_ref, bit):
    return jnp.bitwise_and(lax.shift_right_logical(at_ref[1], bit), 1) == 0


def ordered(low, mine, other):
    return jnp.concatenate([jnp.where(low, mine, other), jnp.where(low, other, mine)], 0)


def start_kernel(at_ref, mine_ref, other_ref, up_ref, half_ref):
    side = jnp.bitwise_and(at_ref[1], 1)
    up = ordered(
        bit_of(at_ref, 0), halve(mine_ref[side, pl.ds(0, BLK)]), halve(other_ref[side, pl.ds(0, BLK)])
    )
    up_ref[...] = up
    half_ref[...] = halve(up)


def climb(bit, at_ref, mine_ref, near_ref, same_ref, cross_ref):
    low = bit_of(at_ref, bit)
    own = ordered(low, halve(mine_ref[...]), halve(near_ref[...]))
    sibling = ordered(low, same_ref[...], cross_ref[...])
    return sibling, ordered(bit_of(at_ref, bit + 1), halve(own), halve(sibling))


def middle_kernel(at_ref, mine_ref, near_ref, same_ref, cross_ref, w_ref, sib_ref, up_ref, half_ref, w_half_ref):
    sib_ref[...], up = climb(1, at_ref, mine_ref, near_ref, same_ref, cross_ref)
    up_ref[...] = up
    half_ref[...] = halve(up)
    core = jnp.bitwise_and(at_ref[1], 1)
    w_half_ref[...] = w_ref[pl.ds(pl.multiple_of(core * 128, 128), 128)]


def last_kernel(at_ref, mine_ref, near_ref, same_ref, cross_ref, p5_ref, p6_ref, up_ref, held_ref):
    held_ref[0], held_ref[1], held_ref[2] = p5_ref[...], p6_ref[...], near_ref[...]
    held_ref[3], up_ref[...] = climb(3, at_ref, mine_ref, near_ref, same_ref, cross_ref)


def near_chunk(by, shards, at_ref, q_ref, lev_ref, face_ref, back_ref, o_ref, l_ref, m_ref):
    chunk, place = jnp.bitwise_and(at_ref[0] + by, 3), at_ref[1]
    even = jnp.bitwise_and(place, 1) == 0

    def panel(ref, side, start, rows=BLK):
        return ref[side, pl.ds(pl.multiple_of(start, BLK), rows)]
    for t in range(2):
        base = chunk * CHUNK + t * 256
        q = q_ref[pl.ds(pl.multiple_of(base, 256), 256)]
        parts = []
        for side in range(2):
            main = jnp.concatenate([
                panel(lev_ref, side, base, 256),
                panel(lev_ref, side, 2048 + chunk * 256 + (1 - t) * BLK),
                panel(lev_ref, side, 3072 + jnp.bitwise_xor(chunk, 1) * BLK)], 0)
            third = panel(lev_ref, side, 3584 + jnp.bitwise_xor(lax.shift_right_logical(chunk, 1), 1) * BLK)
            if t == 0:
                low = panel(lev_ref, side, jnp.maximum(base - BLK, 0))
                halo = jnp.where(even, back_ref[side], face_ref[side, pl.ds(BLK, BLK)])
                low = jnp.where(chunk == 0, halo, low)
                high = panel(lev_ref, side, base + 256)
            else:
                low = panel(lev_ref, side, base - BLK)
                high = panel(lev_ref, side, jnp.minimum(base + 256, 2048 - BLK))
                halo = jnp.where(even, face_ref[side, pl.ds(BLK, BLK)], back_ref[side])
                high = jnp.where(chunk == 3, halo, high)
            parts.append((main, jnp.concatenate([third, low], 0), jnp.concatenate([third, high], 0)))
        ks, vs = parts
        for pair in range(2):
            h0, h1 = spread(q, pair)
            qs = jnp.concatenate([h0[:128], h1[:128], h0[128:], h1[128:]], 0)
            k1, k2, k3 = [twice(k, pair) for k in ks]
            v1, v2, v3 = [ones_beside(v, pair) for v in vs]
            s1 = scores(qs, k1)
            s2 = scores(qs[:256], k2)
            s3 = scores(qs[256:], k3)
            if t == 0:
                bias = jnp.where((chunk == 0) & (place == 0), HIDE, 0.0)
                s2 = jnp.concatenate([s2[:, :128], s2[:, 128:] + bias], 1)
            else:
                bias = jnp.where((chunk == 3) & (place == shards - 1), HIDE, 0.0)
                s3 = jnp.concatenate([s3[:, :128], s3[:, 128:] + bias], 1)
            s23 = jnp.concatenate([s2, s3], 0)
            m = jnp.max(jnp.concatenate([s1, s23], 1), axis=1, keepdims=True)
            p1 = jnp.exp2(s1 - m).astype(BF16)
            p23 = jnp.exp2(s23 - m).astype(BF16)
            o = jnp.dot(p1, v1, preferred_element_type=F32)
            o = o + jnp.concatenate([jnp.dot(p23[:256], v2, preferred_element_type=F32),
                                     jnp.dot(p23[256:], v3, preferred_element_type=F32)], 0)
            for part in range(2):
                r = part * 256
                rows = pl.ds(t * 256 + part * 128, 128)
                cols = pl.ds(pair * 128, 128)
                o_ref[rows, cols] = select(o[r:r+128, :128], o[r+128:r+256, :128])
                l_ref[rows, cols] = select(o[r:r+128, 128:], o[r+128:r+256, 128:])
                m_ref[rows, cols] = select(m[r:r+128], m[r+128:r+256])


def near_kernel(turns, shards, *refs):
    for i, by in enumerate(turns):
        near_chunk(by, shards, *refs[:5], *refs[5 + 3 * i : 8 + 3 * i])


def far_kernel(by, at_ref, q_ref, o_ref, l_ref, m_ref, face_ref, mine_ref, other_ref, mine9_ref, other9_ref, out_ref):
    chunk, core = jnp.bitwise_and(at_ref[0] + by, 3), jnp.bitwise_and(at_ref[1], 1)
    q = q_ref[pl.ds(pl.multiple_of(chunk * CHUNK, CHUNK), CHUNK)]
    mine, other = [
        jnp.concatenate([four[...].reshape(4 * BLK, WIDE), last[...]], 0)
        for four, last in ((mine_ref, mine9_ref), (other_ref, other9_ref))
    ]
    k = jnp.concatenate([face_ref[0, pl.ds(0, BLK)], jnp.where(core == 0, mine, other)], 0)
    v = jnp.concatenate([face_ref[1, pl.ds(0, BLK)], jnp.where(core == 0, other, mine)], 0)
    for pair in range(2):
        k1, v1 = twice(k, pair), ones_beside(v, pair)
        sums, tops = [], []
        for qh in spread(q, pair):
            s = scores(qh, k1)
            m = jnp.max(s, axis=1, keepdims=True)
            sums.append(jnp.dot(jnp.exp2(s - m).astype(BF16), v1, preferred_element_type=F32))
            tops.append(m)
        cols = pl.ds(pair * 128, 128)
        o = select(sums[0][:, :128], sums[1][:, :128])
        l = select(sums[0][:, 128:], sums[1][:, 128:])
        m = select(*tops)
        before = m_ref[:, cols]
        top = jnp.maximum(m, before)
        a, b = jnp.exp2(before - top), jnp.exp2(m - top)
        out = (o * b + o_ref[:, cols] * a) / (l * b + l_ref[:, cols] * a)
        out_ref[:, cols] = out.astype(BF16)


def times(at_ref, att_ref, mine_ref, other_ref):
    first = jnp.bitwise_and(at_ref[1], 1) == 0
    return jnp.dot(
        att_ref[...], ordered(first, mine_ref[...], other_ref[...]), preferred_element_type=F32
    )


def project_kernel(at_ref, own_ref, w_own_ref, a_ref, mine_ref, other_ref, sum_ref):
    total = jnp.dot(own_ref[...], w_own_ref[...], preferred_element_type=F32)
    sum_ref[...] = total + times(at_ref, a_ref, mine_ref, other_ref)


def finish_kernel(at_ref, sum_ref, *refs):
    total = times(at_ref, *refs[:3]) + times(at_ref, *refs[3:6])
    refs[6][...] = (sum_ref[...] + total).astype(BF16)


def body(queries, keys_values, out_weight):
    shards = lax.axis_size("ctx")
    heads = lax.axis_size("head")
    place = lax.axis_index("ctx")
    rank = lax.axis_index("head")
    at = jnp.stack([rank, place]).astype(jnp.int32)
    barrier = lax.optimization_barrier

    def swap(x, bits):
        return lax.ppermute(x, "ctx", [(i, i ^ bits) for i in range(shards)])

    def turn(x, by):
        return lax.ppermute(x, "head", [(i, (i + by) % heads) for i in range(heads)])

    panel, half = ((BLK, WIDE), BF16), ((BLK // 2, WIDE), BF16)
    levels, face, back = call(
        pyramid_kernel,
        "pyramid",
        [((2, 3840, WIDE), BF16), ((2, 2 * BLK, WIDE), BF16), ((2, BLK, WIDE), BF16)],
        (at, keys_values, queries),
    )
    turns = (2, 1, 3, 0)
    sibling = swap(face, 1)
    ends = [(i, i + 1) for i in range(1, shards - 1, 2)]
    back = lax.ppermute(back, "ctx", ends + [(b, a) for a, b in ends])

    def near(chunks, gate):
        return call(
            functools.partial(near_kernel, [turns[i] for i in chunks], shards),
            "near",
            [((CHUNK, WIDE), F32)] * (3 * len(chunks)),
            (at, queries, levels, sibling, back),
            (gate,),
        )

    def exchange(up, part, bit):
        return swap(up, 1 << bit), swap(part, 2 << bit), swap(part, 3 << bit)

    up5, part6 = call(start_kernel, "start", [panel, half], (at, face, sibling))
    got = exchange(up5, part6, 1)
    near0 = near((0,), up5)
    *got, near0[0] = barrier((*got, near0[0]))
    p6, up7, part8, w_half = call(
        middle_kernel,
        "middle",
        [panel, panel, half, ((128, 1024), BF16)],
        (at, up5, *got, out_weight),
    )
    p5 = got[0]
    got = exchange(up7, part8, 3)
    near1 = near((1,), up7)
    *got, near1[0] = barrier((*got, near1[0]))
    w2 = turn(w_half, 2)
    up9, held = call(last_kernel, "last", [panel, ((4, BLK, WIDE), BF16)], (at, up7, *got, p5, p6))
    p9 = swap(up9, 56)
    theirs = swap(held, 1)
    near23 = near((2, 3), up9)
    p9, near23[0] = barrier((p9, near23[0]))
    near2, near3 = near23[:3], near23[3:]
    theirs9 = swap(p9, 1)
    w2, source = barrier((w2, w_half))
    w_mine = [w2, turn(source, 1), turn(source, 3)]
    w_other = [swap(w, 1) for w in w_mine]
    atts = []
    for by, state in zip(turns, (near0, near1, near2, near3)):
        (att,) = call(
            functools.partial(far_kernel, by),
            "far",
            [((CHUNK, WIDE), BF16)],
            (at, queries, *state, sibling, held, theirs, p9, theirs9),
        )
        atts.append(turn(att, by) if by else att)
    pieces = list(zip(atts, w_mine, w_other))
    (part,) = call(
        project_kernel, "project", [((CHUNK, 1024), F32)], (at, atts[3], out_weight, *pieces[2])
    )
    (out,) = call(
        finish_kernel, "finish", [((CHUNK, 1024), BF16)], (at, part, *pieces[1], *pieces[0])
    )
    return out


def solution(mesh):
    in_specs = (P("ctx", "head"), P(None, "ctx", "head"), P("head", None))
    out_specs = P(("ctx", "head"), None)
    return jax.shard_map(body, mesh=mesh, in_specs=in_specs, out_specs=out_specs, check_vma=False)
```

```python
import functools
import math

import jax
import jax.numpy as jnp
from jax import lax
from jax.experimental import pallas as pl
from jax.experimental.pallas import tpu as pltpu
from jax.sharding import PartitionSpec as P

HD = 64
BLK = 128
WIDE = 256
CHUNK = 512
SCALE = math.log2(math.e) / math.sqrt(HD)
ROOT = 1.0 / math.sqrt(2.0)
HIDE = -1e30
NT = (((1,), (1,)), ((), ()))
F32 = jnp.float32
BF16 = jnp.bfloat16

VMEM = pl.BlockSpec(memory_space=pltpu.VMEM)
SMEM = pl.BlockSpec(memory_space=pltpu.SMEM)


def call(kernel, name, outs, args, after=(), limit=16):
    n, late = len(args), len(after)
    return list(
        pl.pallas_call(
            lambda *refs: kernel(*refs[:n], *refs[n + late :]),
            out_shape=[jax.ShapeDtypeStruct(shape, dtype) for shape, dtype in outs],
            in_specs=[SMEM] + [VMEM] * (n - 1) + [pl.BlockSpec(memory_space=pl.ANY)] * late,
            out_specs=[VMEM] * len(outs),
            compiler_params=pltpu.CompilerParams(vmem_limit_bytes=limit * 2**20),
            name=name,
        )(*args, *after)
    )


def halve(rows):
    n = rows.shape[0]
    out = lax.broadcasted_iota(jnp.int32, (n // 2, n), 0)
    col = lax.broadcasted_iota(jnp.int32, (n // 2, n), 1)
    pairs = (col // 2 == out).astype(BF16)
    return (jnp.dot(pairs, rows, preferred_element_type=F32) * ROOT).astype(BF16)


def spread(q, pair):
    x = q[:, pair * 128 : pair * 128 + 128].astype(F32) * SCALE
    head = x.astype(BF16)
    rest = (x - head.astype(F32)).astype(BF16)
    low = lax.broadcasted_iota(jnp.int32, head.shape, 1) < HD
    zero = jnp.zeros_like(head)
    return [
        jnp.concatenate([jnp.where(keep, head, zero), jnp.where(keep, rest, zero)], 1)
        for keep in (low, jnp.logical_not(low))
    ]


def twice(k, pair):
    k = k[:, pair * 128 : pair * 128 + 128]
    return jnp.concatenate([k, k], 1)


def ones_beside(v, pair):
    v = v[:, pair * 128 : pair * 128 + 128]
    return jnp.concatenate([v, jnp.ones_like(v)], 1)


def scores(q, k):
    return lax.dot_general(q, k, NT, preferred_element_type=F32)


def select(x0, x1):
    low = lax.broadcasted_iota(jnp.int32, (x0.shape[0], 128), 1) < HD
    return jnp.where(low, x0, x1)


def pyramid_kernel(at_ref, kv_ref, lev_ref, face_ref, back_ref):
    even = jnp.bitwise_and(at_ref[1], 1) == 0
    for side in range(2):
        for i in range(8):
            rows = kv_ref[side, pl.ds(i * 256, 256)]
            lev_ref[side, pl.ds(i * 256, 256)] = rows
            lev_ref[side, pl.ds(2048 + i * 128, 128)] = halve(rows)
        first, last = kv_ref[side, pl.ds(0, BLK)], kv_ref[side, pl.ds(2048 - BLK, BLK)]
        face_ref[side, pl.ds(BLK, BLK)] = jnp.where(even, last, first)
        back_ref[side] = jnp.where(even, first, last)
    for side in range(2):
        for i in range(4):
            lev_ref[side, pl.ds(3072 + i * 128, 128)] = halve(lev_ref[side, pl.ds(2048 + i * 256, 256)])
    for side in range(2):
        for i in range(2):
            lev_ref[side, pl.ds(3584 + i * 128, 128)] = halve(lev_ref[side, pl.ds(3072 + i * 256, 256)])
    for side in range(2):
        face_ref[side, pl.ds(0, BLK)] = halve(lev_ref[side, pl.ds(3584, 256)])


def bit_of(at_ref, bit):
    return jnp.bitwise_and(lax.shift_right_logical(at_ref[1], bit), 1) == 0


def ordered(low, mine, other):
    return jnp.concatenate([jnp.where(low, mine, other), jnp.where(low, other, mine)], 0)


def start_kernel(at_ref, mine_ref, other_ref, up_ref, half_ref):
    side = jnp.bitwise_and(at_ref[1], 1)
    up = ordered(
        bit_of(at_ref, 0), halve(mine_ref[side, pl.ds(0, BLK)]), halve(other_ref[side, pl.ds(0, BLK)])
    )
    up_ref[...] = up
    half_ref[...] = halve(up)


def climb(bit, at_ref, mine_ref, near_ref, same_ref, cross_ref):
    low = bit_of(at_ref, bit)
    own = ordered(low, halve(mine_ref[...]), halve(near_ref[...]))
    sibling = ordered(low, same_ref[...], cross_ref[...])
    return sibling, ordered(bit_of(at_ref, bit + 1), halve(own), halve(sibling))


def middle_kernel(at_ref, mine_ref, near_ref, same_ref, cross_ref, w_ref, sib_ref, up_ref, half_ref, w_half_ref):
    sib_ref[...], up = climb(1, at_ref, mine_ref, near_ref, same_ref, cross_ref)
    up_ref[...] = up
    half_ref[...] = halve(up)
    core = jnp.bitwise_and(at_ref[1], 1)
    w_half_ref[...] = w_ref[pl.ds(pl.multiple_of(core * 128, 128), 128)]


def last_kernel(at_ref, mine_ref, near_ref, same_ref, cross_ref, p5_ref, p6_ref, up_ref, held_ref):
    held_ref[0], held_ref[1], held_ref[2] = p5_ref[...], p6_ref[...], near_ref[...]
    held_ref[3], up_ref[...] = climb(3, at_ref, mine_ref, near_ref, same_ref, cross_ref)


def near_chunk(by, shards, at_ref, q_ref, lev_ref, face_ref, back_ref, o_ref, l_ref, m_ref):
    chunk, place = jnp.bitwise_and(at_ref[0] + by, 3), at_ref[1]
    even = jnp.bitwise_and(place, 1) == 0

    def panel(ref, side, start, rows=BLK):
        return ref[side, pl.ds(pl.multiple_of(start, BLK), rows)]
    for t in range(2):
        base = chunk * CHUNK + t * 256
        q = q_ref[pl.ds(pl.multiple_of(base, 256), 256)]
        parts = []
        for side in range(2):
            main = jnp.concatenate([
                panel(lev_ref, side, base, 256),
                panel(lev_ref, side, 2048 + chunk * 256 + (1 - t) * BLK),
                panel(lev_ref, side, 3072 + jnp.bitwise_xor(chunk, 1) * BLK)], 0)
            third = panel(lev_ref, side, 3584 + jnp.bitwise_xor(lax.shift_right_logical(chunk, 1), 1) * BLK)
            if t == 0:
                low = panel(lev_ref, side, jnp.maximum(base - BLK, 0))
                halo = jnp.where(even, back_ref[side], face_ref[side, pl.ds(BLK, BLK)])
                low = jnp.where(chunk == 0, halo, low)
                high = panel(lev_ref, side, base + 256)
            else:
                low = panel(lev_ref, side, base - BLK)
                high = panel(lev_ref, side, jnp.minimum(base + 256, 2048 - BLK))
                halo = jnp.where(even, face_ref[side, pl.ds(BLK, BLK)], back_ref[side])
                high = jnp.where(chunk == 3, halo, high)
            parts.append((main, jnp.concatenate([third, low], 0), jnp.concatenate([third, high], 0)))
        ks, vs = parts
        for pair in range(2):
            h0, h1 = spread(q, pair)
            qs = jnp.concatenate([h0[:128], h1[:128], h0[128:], h1[128:]], 0)
            k1, k2, k3 = [twice(k, pair) for k in ks]
            v1, v2, v3 = [ones_beside(v, pair) for v in vs]
            s1 = scores(qs, k1)
            s2 = scores(qs[:256], k2)
            s3 = scores(qs[256:], k3)
            if t == 0:
                bias = jnp.where((chunk == 0) & (place == 0), HIDE, 0.0)
                s2 = jnp.concatenate([s2[:, :128], s2[:, 128:] + bias], 1)
            else:
                bias = jnp.where((chunk == 3) & (place == shards - 1), HIDE, 0.0)
                s3 = jnp.concatenate([s3[:, :128], s3[:, 128:] + bias], 1)
            s23 = jnp.concatenate([s2, s3], 0)
            m = jnp.max(jnp.concatenate([s1, s23], 1), axis=1, keepdims=True)
            p1 = jnp.exp2(s1 - m).astype(BF16)
            p23 = jnp.exp2(s23 - m).astype(BF16)
            o = jnp.dot(p1, v1, preferred_element_type=F32)
            o = o + jnp.concatenate([jnp.dot(p23[:256], v2, preferred_element_type=F32),
                                     jnp.dot(p23[256:], v3, preferred_element_type=F32)], 0)
            for part in range(2):
                r = part * 256
                rows = pl.ds(t * 256 + part * 128, 128)
                cols = pl.ds(pair * 128, 128)
                o_ref[rows, cols] = select(o[r:r+128, :128], o[r+128:r+256, :128])
                l_ref[rows, cols] = select(o[r:r+128, 128:], o[r+128:r+256, 128:])
                m_ref[rows, cols] = select(m[r:r+128], m[r+128:r+256])


def near_kernel(turns, shards, *refs):
    for i, by in enumerate(turns):
        near_chunk(by, shards, *refs[:5], *refs[5 + 3 * i : 8 + 3 * i])


def far_kernel(by, at_ref, q_ref, o_ref, l_ref, m_ref, face_ref, mine_ref, other_ref, mine9_ref, other9_ref, out_ref):
    chunk, core = jnp.bitwise_and(at_ref[0] + by, 3), jnp.bitwise_and(at_ref[1], 1)
    q = q_ref[pl.ds(pl.multiple_of(chunk * CHUNK, CHUNK), CHUNK)]
    mine, other = [
        jnp.concatenate([four[...].reshape(4 * BLK, WIDE), last[...]], 0)
        for four, last in ((mine_ref, mine9_ref), (other_ref, other9_ref))
    ]
    k = jnp.concatenate([face_ref[0, pl.ds(0, BLK)], jnp.where(core == 0, mine, other)], 0)
    v = jnp.concatenate([face_ref[1, pl.ds(0, BLK)], jnp.where(core == 0, other, mine)], 0)
    for pair in range(2):
        k1, v1 = twice(k, pair), ones_beside(v, pair)
        sums, tops = [], []
        for qh in spread(q, pair):
            s = scores(qh, k1)
            m = jnp.max(s, axis=1, keepdims=True)
            sums.append(jnp.dot(jnp.exp2(s - m).astype(BF16), v1, preferred_element_type=F32))
            tops.append(m)
        cols = pl.ds(pair * 128, 128)
        o = select(sums[0][:, :128], sums[1][:, :128])
        l = select(sums[0][:, 128:], sums[1][:, 128:])
        m = select(*tops)
        before = m_ref[:, cols]
        top = jnp.maximum(m, before)
        a, b = jnp.exp2(before - top), jnp.exp2(m - top)
        out = (o * b + o_ref[:, cols] * a) / (l * b + l_ref[:, cols] * a)
        out_ref[:, cols] = out.astype(BF16)


def times(at_ref, att_ref, mine_ref, other_ref):
    first = jnp.bitwise_and(at_ref[1], 1) == 0
    return jnp.dot(
        att_ref[...], ordered(first, mine_ref[...], other_ref[...]), preferred_element_type=F32
    )


def project_kernel(at_ref, own_ref, w_own_ref, *refs):
    total = jnp.dot(own_ref[...], w_own_ref[...], preferred_element_type=F32)
    for i in range(3):
        total = total + times(at_ref, *refs[3 * i : 3 * i + 3])
    refs[9][...] = total.astype(BF16)


def body(queries, keys_values, out_weight):
    shards = lax.axis_size("ctx")
    heads = lax.axis_size("head")
    place = lax.axis_index("ctx")
    rank = lax.axis_index("head")
    at = jnp.stack([rank, place]).astype(jnp.int32)
    barrier = lax.optimization_barrier

    def swap(x, bits):
        return lax.ppermute(x, "ctx", [(i, i ^ bits) for i in range(shards)])

    def turn(x, by):
        return lax.ppermute(x, "head", [(i, (i + by) % heads) for i in range(heads)])

    panel, half = ((BLK, WIDE), BF16), ((BLK // 2, WIDE), BF16)
    levels, face, back = call(
        pyramid_kernel,
        "pyramid",
        [((2, 3840, WIDE), BF16), ((2, 2 * BLK, WIDE), BF16), ((2, BLK, WIDE), BF16)],
        (at, keys_values),
    )
    turns = (2, 1, 3, 0)
    sibling = swap(face, 1)
    ends = [(i, i + 1) for i in range(1, shards - 1, 2)]
    back = lax.ppermute(back, "ctx", ends + [(b, a) for a, b in ends])

    def near(chunks, gate):
        return call(
            functools.partial(near_kernel, [turns[i] for i in chunks], shards),
            "near",
            [((CHUNK, WIDE), F32)] * (3 * len(chunks)),
            (at, queries, levels, sibling, back),
            (gate,),
        )

    def exchange(up, part, bit):
        return swap(up, 1 << bit), swap(part, 2 << bit), swap(part, 3 << bit)

    up5, part6 = call(start_kernel, "start", [panel, half], (at, face, sibling))
    got = exchange(up5, part6, 1)
    near0 = near((0,), up5)
    *got, near0[0] = barrier((*got, near0[0]))
    p6, up7, part8, w_half = call(
        middle_kernel,
        "middle",
        [panel, panel, half, ((128, 1024), BF16)],
        (at, up5, *got, out_weight),
    )
    p5 = got[0]
    got = exchange(up7, part8, 3)
    near1 = near((1,), up7)
    *got, near1[0] = barrier((*got, near1[0]))
    w2 = turn(w_half, 2)
    up9, held = call(last_kernel, "last", [panel, ((4, BLK, WIDE), BF16)], (at, up7, *got, p5, p6))
    p9 = swap(up9, 56)
    theirs = swap(held, 1)
    near23 = near((2, 3), up9)
    p9, near23[0] = barrier((p9, near23[0]))
    near2, near3 = near23[:3], near23[3:]
    theirs9 = swap(p9, 1)
    w2, source = barrier((w2, w_half))
    w_mine = [w2, turn(source, 1), turn(source, 3)]
    w_other = [swap(w, 1) for w in w_mine]
    atts = []
    for by, state in zip(turns, (near0, near1, near2, near3)):
        (att,) = call(
            functools.partial(far_kernel, by),
            "far",
            [((CHUNK, WIDE), BF16)],
            (at, queries, *state, sibling, held, theirs, p9, theirs9),
        )
        atts.append(turn(att, by) if by else att)
    pieces = list(zip(atts, w_mine, w_other))
    (out,) = call(
        project_kernel,
        "project",
        [((CHUNK, 1024), BF16)],
        (at, atts[3], out_weight, *pieces[2], *pieces[1], *pieces[0]),
    )
    return out


def solution(mesh):
    in_specs = (P("ctx", "head"), P(None, "ctx", "head"), P("head", None))
    out_specs = P(("ctx", "head"), None)
    return jax.shard_map(body, mesh=mesh, in_specs=in_specs, out_specs=out_specs, check_vma=False)
```
